512 devices in a mesh: dp: 64 (over y, z), tp: 8 (over x, core).
Axes of the slice: x: 4, y: 8, z: 8, core: 2. Of those that a mesh axis runs over, the one named last changes fastest.
Arguments:
- hidden: bfloat16 [256, 7168], P('dp', 'tp'), may hold values from -6 to 6
- kva_weight: bfloat16 [7168, 576], P('tp'), may hold values from -0.0625 to 0.0625
- kv_gain: float32 [512], replicated, may hold values from 0.5 to 1.5
- queries: bfloat16 [256, 128, 576], P('dp')
- latent_cache: bfloat16 [6144, 64, 576], P('dp', 'tp'), may hold values from -6 to 6
- outbox: bfloat16 [4096, 64, 576], P('dp', 'tp'), may hold values from -6 to 6
- out_dest: int32 [4096], P('dp'), may hold values from 0 to 63, as said below
- page_table: int32 [256, 40], P('dp'), may hold values from 0 to 223, as said below
- lengths: int32 [256], P('dp'), may hold values from 1025 to 2560, as said below
- give_rows: int32 [128], P('dp'), may hold values from 0 to 3, as said below
Outputs:
- attended: bfloat16 [256, 128, 512], P('dp', 'tp')
- new_latent: bfloat16 [256, 576], P('dp')
The draws below stay inside these ranges and needn't reach their ends.
Inputs may be any that keep to these rules, and one draw needn't show every extreme that they name: `out_dest`: no group sends more than 2 pages to one group; every group sends exactly 2 pages to some group. `page_table`: each row lists its resident pages (entries below 96, no resident page in two rows of a group), then exactly 16 filled arrival slots (entry 96 + s * 2 + k), then entries that its length leaves unused; every request has at least one full resident page. `lengths`: tokens covered: all listed pages but the last arrived one are full; some row of each group has the full 40 * 64. `give_rows`: 2 different rows of each group.
All inputs are finite; a program needn't handle non-finite values.
Results may differ from the reference program's by a relative error of at most 0.012.
Values may be sent and summed in bfloat16 or wider, within the bound.
No kernel may reach another device: no remote copies, remote signals or barrier semaphores. Data moves between devices by JAX's collectives and lax.ppermute only.
A program may use at most 64 MiB of HBM per device.

```python
import jax
import jax.numpy as jnp
from jax import lax

D = 7168
HEADS = 128
KVL = 512
LAT = 576
PAGE = 64
CAP = 2
MOVES = 2
ROWS = 4
RESMAX = 24
GROUPS = 64
NP = 64
ARR = 16
MAXP = 40
RES_POOL = 96
N_TP = 8


def plan(key):
    keys = jax.random.split(key, 8)
    ranking = jax.random.permutation(keys[0], GROUPS)
    counts = jnp.where(ranking < GROUPS // 4, CAP, jnp.where(ranking < 3 * GROUPS // 4, CAP // 2, 0)).astype(jnp.int32)
    offset_grid = jnp.repeat(jnp.arange(GROUPS, dtype=jnp.int32), CAP)
    copy_grid = jnp.tile(jnp.arange(CAP, dtype=jnp.int32), GROUPS)
    slot_ids = jnp.arange(GROUPS * CAP, dtype=jnp.int32)
    usable = copy_grid < counts[offset_grid]
    ordering = jnp.argsort(jnp.where(usable, 0, 1) * (GROUPS * CAP) + slot_ids, stable=True)
    offsets = offset_grid[ordering[:NP]]
    shuffles = jax.vmap(lambda sub: jax.random.permutation(sub, NP))(jax.random.split(keys[1], GROUPS))
    group_ids = jnp.arange(GROUPS, dtype=jnp.int32)
    out_dest = (group_ids[:, None] + offsets[shuffles]) % GROUPS
    filled = copy_grid[None, :] < counts[(group_ids[:, None] - offset_grid[None, :]) % GROUPS]
    compact = jnp.argsort(jnp.where(filled, 0, 1) * (GROUPS * CAP) + slot_ids[None, :], axis=1, stable=True)[:, :NP]
    mixing = jax.vmap(lambda sub: jax.random.permutation(sub, NP))(jax.random.split(keys[2], GROUPS))
    arrivals = (jnp.take_along_axis(compact, mixing, axis=1) + RES_POOL).astype(jnp.int32).reshape(GROUPS, ROWS, ARR)
    resident = jax.vmap(lambda sub: jax.random.permutation(sub, RES_POOL))(jax.random.split(keys[3], GROUPS))
    resident = resident.astype(jnp.int32).reshape(GROUPS, ROWS, RESMAX)
    res_counts = jax.random.randint(keys[4], (GROUPS, ROWS), 1, RESMAX + 1)
    forced = jax.random.randint(keys[5], (GROUPS, 1), 0, ROWS)
    is_forced = jnp.arange(ROWS)[None, :] == forced
    res_counts = jnp.where(is_forced, RESMAX, res_counts)
    column = jnp.broadcast_to(jnp.arange(MAXP, dtype=jnp.int32)[None, None, :], (GROUPS, ROWS, MAXP))
    from_res = jnp.take_along_axis(resident, jnp.minimum(column, RESMAX - 1), axis=2)
    from_arr = jnp.take_along_axis(arrivals, jnp.clip(column - res_counts[..., None], 0, ARR - 1), axis=2)
    mapping = jnp.where(column < res_counts[..., None], from_res, jnp.where(column < res_counts[..., None] + ARR, from_arr, 0))
    tail_tokens = jnp.where(is_forced, PAGE, jax.random.randint(keys[6], (GROUPS, ROWS), 1, PAGE + 1))
    lengths = (res_counts + ARR - 1) * PAGE + tail_tokens
    given = jax.vmap(lambda sub: jax.random.permutation(sub, ROWS))(jax.random.split(keys[7], GROUPS))[:, :MOVES]
    return (out_dest.reshape(-1).astype(jnp.int32), mapping.reshape(GROUPS * ROWS, MAXP).astype(jnp.int32), lengths.reshape(-1).astype(jnp.int32), given.reshape(-1).astype(jnp.int32))


def draw_out_dest(key, part):
    return plan(key)[0]


def draw_page_table(key, part):
    return plan(key)[1]


def draw_lengths(key, part):
    return plan(key)[2]


def draw_give_rows(key, part):
    return plan(key)[3]


def draw_queries(key, part):
    key = jax.random.fold_in(key, 11)
    first = jax.random.fold_in(key, 0)
    shape = (GROUPS * ROWS, HEADS, LAT)
    return jax.random.normal(first, shape, jnp.float32).astype(jnp.bfloat16)


def block_scale(rng, dims, cuts, smallest, largest):
    factor_of, own = 1.0, jax.random.fold_in(rng, 6)
    for dim, blocks in cuts:
        steps = jnp.exp(jax.random.uniform(jax.random.fold_in(own, dim), (blocks,), jnp.float32, smallest / len(cuts), largest / len(cuts)))
        factor_of = factor_of * jnp.repeat(steps, dims[dim] // blocks).reshape([-1 if axis == dim else 1 for axis in range(len(dims))])
    return factor_of


def normal_values(stream_key, dims, deviation, reach, cuts=(), kind=jnp.bfloat16):
    factor_of = block_scale(stream_key, dims, cuts, -0.22, 0.18) if cuts else 1.0
    entries = jax.random.normal(stream_key, dims, jnp.float32) * deviation * factor_of
    return jnp.minimum(jnp.maximum(entries, -reach), reach).astype(kind)


def setup_inputs(seed: int = 0) -> dict:
    key_list = jax.random.split(jax.random.key(seed), 11)
    hidden = normal_values(key_list[0], (GROUPS * ROWS, D), 1.0, 6.0, ((0, 64), (1, 8)))
    kva_weight = normal_values(key_list[1], (D, LAT), D ** -0.5, 0.0625, ((0, 8),))
    kv_gain = jnp.clip(1.0 + 0.1 * jax.random.normal(key_list[2], (KVL,), jnp.float32), 0.5, 1.5)
    queries = draw_queries(jax.random.fold_in(key_list[10], 71), 0)
    latent_cache = normal_values(key_list[4], (GROUPS * RES_POOL, PAGE, LAT), 1.0, 6.0, ((0, 64), (1, 8)))
    outbox = normal_values(key_list[5], (GROUPS * NP, PAGE, LAT), 1.0, 6.0, ((0, 64), (1, 8)))
    out_dest = draw_out_dest(jax.random.fold_in(key_list[10], 71), 0)
    page_table = draw_page_table(jax.random.fold_in(key_list[10], 71), 0)
    lengths = draw_lengths(jax.random.fold_in(key_list[10], 71), 0)
    give_rows = draw_give_rows(jax.random.fold_in(key_list[10], 71), 0)
    return dict(hidden=hidden, kva_weight=kva_weight, kv_gain=kv_gain, queries=queries, latent_cache=latent_cache, outbox=outbox, out_dest=out_dest, page_table=page_table, lengths=lengths, give_rows=give_rows)


EPSILON = 1e-06
SCORE_SCALE = 192.0 ** (-0.5)

def arrival_map(out_dest):
    dest_rows = out_dest.reshape(GROUPS, NP)
    same_dest = (dest_rows[:, :, None] == dest_rows[:, None, :]).astype(jnp.int32)
    lower_mask = (jnp.arange(NP)[:, None] > jnp.arange(NP)[None, :]).astype(jnp.int32)
    dest_rank = lax.optimization_barrier(jnp.sum(same_dest * lower_mask[None], axis=2)).astype(jnp.int32)
    source_ids = jnp.arange(GROUPS, dtype=jnp.int32)[:, None] * jnp.ones((1, NP), jnp.int32)
    columns = source_ids * CAP + dest_rank
    flat_ids = source_ids * NP + jnp.arange(NP, dtype=jnp.int32)[None, :]
    mapping = jnp.full((GROUPS, GROUPS * CAP), -1, jnp.int32)
    return mapping.at[dest_rows.reshape(-1), columns.reshape(-1)].set(flat_ids.reshape(-1))

def normalize(raw_latent, kv_gain):
    head_part = raw_latent[:, :KVL]
    inverse = lax.rsqrt(lax.optimization_barrier(jnp.mean(head_part * head_part, axis=1, keepdims=True)) + EPSILON)
    return jnp.concatenate([head_part * inverse * kv_gain[None, :], raw_latent[:, KVL:]], axis=1).astype(jnp.bfloat16)

def attend(row_queries, fetched, valid, fresh_latent):
    row_count = row_queries.shape[0]
    piece = PAGE // N_TP
    key_rows = fetched.reshape(row_count, MAXP, N_TP, piece, LAT).transpose(0, 2, 1, 3, 4)
    key_rows = key_rows.reshape(row_count, N_TP, MAXP * piece, LAT)
    live_keys = valid.reshape(row_count, MAXP, N_TP, piece).transpose(0, 2, 1, 3).reshape(row_count, N_TP, MAXP * piece)
    query_float = row_queries.astype(jnp.float32)
    key_float = key_rows.astype(jnp.float32)
    scores = SCORE_SCALE * jnp.einsum('rhl,rtkl->rthk', query_float, key_float)
    scores = jnp.where(live_keys[:, :, None, :], scores, -jnp.inf)
    share_top = lax.optimization_barrier(jnp.max(scores, axis=3))
    weights = jnp.exp(scores - share_top[..., None])
    share_total = lax.optimization_barrier(jnp.sum(weights, axis=3))
    blend = jnp.einsum('rthk,rtkc->rthc', weights.astype(jnp.bfloat16).astype(jnp.float32), key_float[..., :KVL])
    partial_value = (blend / share_total[..., None]).astype(jnp.bfloat16)
    latent_float = fresh_latent.astype(jnp.float32)
    own_score = SCORE_SCALE * jnp.einsum('rhl,rl->rh', query_float, latent_float)
    peak_score = jnp.maximum(lax.optimization_barrier(jnp.max(share_top, axis=1)), own_score)
    factor = jnp.exp(share_top - peak_score[:, None, :]) * share_total
    fresh_weight = jnp.exp(own_score - peak_score)
    numerator = jnp.einsum('rth,rthc->rhc', factor, partial_value.astype(jnp.float32))
    numerator = numerator + fresh_weight[..., None] * latent_float[:, None, :KVL]
    denominator = lax.optimization_barrier(jnp.sum(factor, axis=1)) + fresh_weight
    return (numerator / denominator[..., None]).astype(jnp.bfloat16)

def reference(hidden, kva_weight, kv_gain, queries, latent_cache, outbox, out_dest, page_table, lengths, give_rows):
    mapping = arrival_map(out_dest)
    given = give_rows.reshape(GROUPS, MOVES)
    group_ids = jnp.arange(GROUPS, dtype=jnp.int32)
    partner_ids = (group_ids + GROUPS // 2) % GROUPS
    target_rows = (group_ids[:, None] * ROWS + given).reshape(-1)
    source_rows = (partner_ids[:, None] * ROWS + given[partner_ids]).reshape(-1)
    anchor = jnp.arange(GROUPS * ROWS, dtype=jnp.int32).at[target_rows].set(source_rows)
    raw_latent = jnp.dot(hidden[anchor], kva_weight, preferred_element_type=jnp.float32)
    new_latent = normalize(raw_latent, kv_gain)
    positions = jnp.arange(MAXP * PAGE, dtype=jnp.int32).reshape(MAXP, PAGE)

    def one_group(group):
        row_ids = lax.dynamic_slice_in_dim(anchor, group * ROWS, ROWS)
        home_group = row_ids // ROWS
        page_ids = page_table[row_ids]
        resident = page_ids < RES_POOL
        res_index = home_group[:, None] * RES_POOL + jnp.minimum(page_ids, RES_POOL - 1)
        arr_index = mapping[home_group[:, None], jnp.maximum(page_ids - RES_POOL, 0)]
        from_cache = latent_cache[res_index]
        from_outbox = outbox[jnp.maximum(arr_index, 0)] * (arr_index >= 0)[..., None, None].astype(jnp.bfloat16)
        fetched = jnp.where(resident[..., None, None], from_cache, from_outbox)
        valid = positions[None] < lengths[row_ids][:, None, None]
        fresh_latent = lax.dynamic_slice_in_dim(new_latent, group * ROWS, ROWS)
        return attend(queries[row_ids], fetched, valid, fresh_latent)
    attended = lax.map(one_group, group_ids)
    return (attended.reshape(GROUPS * ROWS, HEADS, KVL), new_latent)
```

```python
import functools

import jax
import jax.numpy as jnp
from jax import lax
from jax.experimental import pallas as pl
from jax.experimental.pallas import tpu as pltpu
from jax.sharding import PartitionSpec as P

KVL = 512
PAGE = 64
CAP = 2
ARR = 16
RESMAX = 24


EPSILON = 1e-06
SCORE_SCALE = 192.0 ** (-0.5)
VMEM_LIMIT = 32 * 1024 * 1024

SMEM = functools.partial(pl.BlockSpec, memory_space=pltpu.SMEM)
VMEM = functools.partial(pl.BlockSpec, memory_space=pltpu.VMEM)


def normalize(raw_latent, kv_gain):
    head_part = raw_latent[:, :KVL]
    inverse = lax.rsqrt(jnp.mean(head_part * head_part, axis=1, keepdims=True) + EPSILON)
    return jnp.concatenate(
        [head_part * inverse * kv_gain[None, :], raw_latent[:, KVL:]], axis=1
    ).astype(jnp.bfloat16)


def pack_kernel(dest_ref, outbox_ref, out_ref, count_ref):
    groups = out_ref.shape[0]
    out_ref[...] = jnp.zeros_like(out_ref)

    def clear(i, _):
        count_ref[i] = 0
        return 0

    lax.fori_loop(0, groups, clear, 0)

    def place(i, _):
        dest = dest_ref[i]
        rank = count_ref[dest]
        count_ref[dest] = rank + 1
        page = outbox_ref[i]

        @pl.when(rank == 0)
        def _():
            out_ref[dest, :, 0:KVL] = page[:, :KVL]
            out_ref[dest, :, 2 * KVL : 2 * KVL + 64] = page[:, KVL:]

        @pl.when(rank == 1)
        def _():
            out_ref[dest, :, KVL : 2 * KVL] = page[:, :KVL]
            out_ref[dest, :, 2 * KVL + 64 : 2 * KVL + 128] = page[:, KVL:]

        return 0

    lax.fori_loop(0, outbox_ref.shape[0], place, 0)


def resident_kernel(table_ref, length_ref, cache_ref, query_ref, score_ref, value_ref, key_ref):
    piece = cache_ref.shape[1]
    for row in range(query_ref.shape[0]):
        count = (length_ref[row] + (PAGE - 1)) // PAGE - ARR

        def fetch(pair, _):
            parts = []
            for half in range(2):
                entry = pair * 2 + half
                index = table_ref[row, jnp.where(entry < count, entry, 0)]
                parts.append(cache_ref[index])
            start = pl.multiple_of(pair * 2 * piece, 2 * piece)
            key_ref[pl.ds(start, 2 * piece), :] = jnp.concatenate(parts, axis=0)
            return 0

        lax.fori_loop(0, RESMAX // 2, fetch, 0)
        keys = key_ref[...]
        scores = SCORE_SCALE * jnp.dot(keys, query_ref[row], preferred_element_type=jnp.float32)
        token = lax.broadcasted_iota(jnp.int32, scores.shape, 0)
        score_ref[row] = jnp.where(token < count * piece, scores, -jnp.inf)
        value_ref[row] = keys[:, :KVL]


def arrived_kernel(
    shard_ref, table_ref, length_ref, arrived_ref, query_ref, score_ref, value_ref, send_ref, key_ref, rope_ref, stat_ref
):
    shards, piece = send_ref.shape[0], arrived_ref.shape[1]
    rows, _, heads = query_ref.shape
    own = heads // shards
    shard = shard_ref[0]
    stat_ref[...] = jnp.zeros_like(stat_ref)
    for row in range(rows):
        length = length_ref[row]
        count = (length + (PAGE - 1)) // PAGE - ARR

        def fetch(pair, _):
            latents, ropes = [], []
            for half in range(2):
                slot = table_ref[row, count + pair * 2 + half] - 96
                source, rank = slot // CAP, lax.rem(slot, CAP)
                first = pl.multiple_of(rank * KVL, KVL)
                latents.append(arrived_ref[source, :, pl.ds(first, KVL)])
                both = arrived_ref[source, :, 2 * KVL : 2 * KVL + 128]
                lane = lax.broadcasted_iota(jnp.int32, both.shape, 1)
                ropes.append(jnp.where(lane // 64 == rank, both.astype(jnp.float32), 0.0).astype(jnp.bfloat16))
            start = pl.multiple_of(pair * 2 * piece, 2 * piece)
            key_ref[pl.ds(start, 2 * piece), :] = jnp.concatenate(latents, axis=0)
            rope_ref[pl.ds(start, 2 * piece), :] = jnp.concatenate(ropes, axis=0)
            return 0

        lax.fori_loop(0, ARR // 2, fetch, 0)
        keys = key_ref[...]
        query = query_ref[row]
        rope_query = query[KVL:]
        scores = jnp.dot(keys, query[:KVL], preferred_element_type=jnp.float32)
        scores += jnp.dot(
            rope_ref[...], jnp.concatenate([rope_query, rope_query], axis=0), preferred_element_type=jnp.float32
        )
        token = lax.broadcasted_iota(jnp.int32, scores.shape, 0)
        position = (count + token // piece) * PAGE + shard * piece + lax.rem(token, piece)
        scores = jnp.where(position < length, SCORE_SCALE * scores, -jnp.inf)
        resident = score_ref[row]
        top = jnp.maximum(jnp.max(scores, axis=0, keepdims=True), jnp.max(resident, axis=0, keepdims=True))
        arrived_weights = jnp.exp(scores - top)
        resident_weights = jnp.exp(resident - top)
        total = jnp.sum(arrived_weights, axis=0, keepdims=True) + jnp.sum(resident_weights, axis=0, keepdims=True)
        inverse = 1.0 / total
        blend = lax.dot_general(
            (resident_weights * inverse).astype(jnp.bfloat16),
            value_ref[row],
            (((0,), (0,)), ((), ())),
            preferred_element_type=jnp.float32,
        ) + lax.dot_general(
            (arrived_weights * inverse).astype(jnp.bfloat16),
            keys,
            (((0,), (0,)), ((), ())),
            preferred_element_type=jnp.float32,
        )
        partial = blend.astype(jnp.bfloat16)
        for shard_to in range(shards):
            part = partial[shard_to * own : (shard_to + 1) * own]
            for chunk in range(KVL // 128):
                start = (chunk * rows + row) * own
                send_ref[shard_to, start : start + own, :] = part[:, chunk * 128 : (chunk + 1) * 128]
        level = top + jnp.log(total)
        for step in range(3):
            rounded = level.astype(jnp.bfloat16).astype(jnp.float32)
            stat_ref[step * rows + row : step * rows + row + 1, :] = rounded
            level = level - rounded
    stats = stat_ref[...].astype(jnp.bfloat16)
    for shard_to in range(shards):
        send_ref[shard_to, KVL // 128 * rows * own :, :] = stats


def combine_kernel(shard_ref, give_ref, received_ref, latent_ref, query_ref, home_ref, give_out_ref, mix_ref):
    shards = received_ref.shape[0]
    rows, _, heads = query_ref.shape
    own = heads // shards
    stat_base = KVL // 128 * rows * own
    latent = latent_ref[...]
    latent_float = latent.astype(jnp.float32)
    levels = []
    for share in range(shards):
        stats = received_ref[share, stat_base:, :].astype(jnp.float32)
        levels.append(stats[0:rows] + stats[rows : 2 * rows] + stats[2 * rows : 3 * rows])
    own_rows = []
    for row in range(rows):
        own_rows.append(jnp.dot(latent, query_ref[row], preferred_element_type=jnp.float32)[row : row + 1])
    own_score = SCORE_SCALE * jnp.concatenate(own_rows, axis=0)
    peak = own_score
    for level in levels:
        peak = jnp.maximum(peak, level)
    weights = [jnp.exp(level - peak) for level in levels] + [jnp.exp(own_score - peak)]
    total = functools.reduce(lambda a, b: a + b, weights)
    inverse = 1.0 / total
    mixed = jnp.concatenate([w * inverse for w in weights], axis=0)
    mixed = jnp.concatenate([mixed, jnp.zeros((heads - mixed.shape[0], heads), jnp.float32)], axis=0)
    mix_ref[...] = mixed.T
    mine = mix_ref[pl.ds(pl.multiple_of(shard_ref[0] * own, own), own), :]
    for row in range(rows):
        last = shards * rows + row
        for chunk in range(KVL // 128):
            lanes = slice(chunk * 128, (chunk + 1) * 128)
            value = mine[:, last : last + 1] * latent_float[row : row + 1, lanes]
            start = (chunk * rows + row) * own
            for share in range(shards):
                column = share * rows + row
                block = received_ref[share, start : start + own, :].astype(jnp.float32)
                value += mine[:, column : column + 1] * block
            home_ref[row, :, lanes] = value.astype(jnp.bfloat16)
    for move in range(give_out_ref.shape[0]):
        give_out_ref[move] = home_ref[give_ref[move]]


def shards(
    hidden,
    kva_weight,
    kv_gain,
    queries,
    latent_cache,
    outbox,
    out_dest,
    page_table,
    lengths,
    give_rows,
):
    group_count = lax.axis_size("dp")
    shard_count = lax.axis_size("tp")
    shard = lax.axis_index("tp").astype(jnp.int32).reshape(1)
    row_count = hidden.shape[0]
    page_piece = latent_cache.shape[1]
    heads = queries.shape[1]
    own = heads // shard_count
    moves = give_rows.shape[0]
    query_t = jnp.swapaxes(queries, 1, 2)
    params = pltpu.CompilerParams(vmem_limit_bytes=VMEM_LIMIT)

    outgoing = pl.pallas_call(
        pack_kernel,
        out_shape=jax.ShapeDtypeStruct((group_count, page_piece, 2 * KVL + 128), jnp.bfloat16),
        in_specs=[SMEM(), VMEM()],
        out_specs=VMEM(),
        scratch_shapes=[pltpu.SMEM((group_count,), jnp.int32)],
        compiler_params=params,
        name="pack",
    )(out_dest, outbox)
    arrived = lax.all_to_all(outgoing, "dp", split_axis=0, concat_axis=0, tiled=True)

    partial_raw = jnp.dot(hidden, kva_weight, preferred_element_type=jnp.float32)
    parts = lax.all_gather(partial_raw, "tp")
    home_latent = normalize(jnp.sum(parts, axis=0), kv_gain)
    partner = [(i, i ^ (group_count // 2)) for i in range(group_count)]
    is_given = (lax.broadcasted_iota(jnp.int32, (moves, row_count), 1) == give_rows[:, None])
    moved_latent = lax.ppermute(
        jnp.sum(jnp.where(is_given[:, :, None], home_latent[None].astype(jnp.float32), 0.0), axis=1).astype(jnp.bfloat16),
        "dp",
        partner,
    )

    def after_move(home, moved):
        shape = (row_count,) + (1,) * (home.ndim - 1)
        for move in range(moves):
            home = jnp.where(is_given[move].reshape(shape), moved[move][None], home)
        return home

    new_latent = after_move(home_latent, moved_latent)

    scores, values = pl.pallas_call(
        resident_kernel,
        out_shape=(
            jax.ShapeDtypeStruct((row_count, RESMAX * page_piece, heads), jnp.float32),
            jax.ShapeDtypeStruct((row_count, RESMAX * page_piece, KVL), jnp.bfloat16),
        ),
        in_specs=[SMEM(), SMEM(), VMEM(), VMEM()],
        out_specs=(VMEM(), VMEM()),
        scratch_shapes=[pltpu.VMEM((RESMAX * page_piece, latent_cache.shape[2]), jnp.bfloat16)],
        compiler_params=params,
        name="resident",
    )(page_table, lengths, latent_cache, query_t)

    send_rows = KVL // 128 * row_count * own + 16
    outbound = pl.pallas_call(
        arrived_kernel,
        out_shape=jax.ShapeDtypeStruct((shard_count, send_rows, 128), jnp.bfloat16),
        in_specs=[SMEM(), SMEM(), SMEM(), VMEM(), VMEM(), VMEM(), VMEM()],
        out_specs=VMEM(),
        scratch_shapes=[
            pltpu.VMEM((ARR * page_piece, KVL), jnp.bfloat16),
            pltpu.VMEM((ARR * page_piece, 128), jnp.bfloat16),
            pltpu.VMEM((16, heads), jnp.float32),
        ],
        compiler_params=params,
        name="arrived",
    )(shard, page_table, lengths, arrived, query_t, scores, values)
    received = lax.all_to_all(outbound, "tp", split_axis=0, concat_axis=0, tiled=True)

    home, given = pl.pallas_call(
        combine_kernel,
        out_shape=(
            jax.ShapeDtypeStruct((row_count, own, KVL), jnp.bfloat16),
            jax.ShapeDtypeStruct((moves, own, KVL), jnp.bfloat16),
        ),
        in_specs=[SMEM(), SMEM(), VMEM(), VMEM(), VMEM()],
        out_specs=(VMEM(), VMEM()),
        scratch_shapes=[pltpu.VMEM((heads, heads), jnp.float32)],
        compiler_params=params,
        name="combine",
    )(shard, give_rows, received, home_latent, query_t)
    attended = after_move(home, lax.ppermute(given, "dp", partner))
    return (attended, new_latent)


def solution(mesh):
    placed = (
        P("dp", "tp"),
        P("tp", None),
        P(),
        P("dp", None, None),
        P("dp", "tp", None),
        P("dp", "tp", None),
        P("dp"),
        P("dp", None),
        P("dp"),
        P("dp"),
    )
    return jax.shard_map(
        shards,
        mesh=mesh,
        in_specs=placed,
        out_specs=(P("dp", "tp", None), P("dp", None)),
        check_vma=False,
    )
```

```python
import functools

import jax
import jax.numpy as jnp
from jax import lax
from jax.experimental import pallas as pl
from jax.experimental.pallas import tpu as pltpu
from jax.sharding import PartitionSpec as P

KVL = 512
PAGE = 64
CAP = 2
ARR = 16
RESMAX = 24
MAXROWS = 4
MOVES = 2
ROPE = 64
RES_POOL = 96


EPSILON = 1e-06
SCORE_SCALE = 192.0 ** (-0.5)
VMEM_LIMIT = 32 * 1024 * 1024

SMEM = functools.partial(pl.BlockSpec, memory_space=pltpu.SMEM)
VMEM = functools.partial(pl.BlockSpec, memory_space=pltpu.VMEM)


def normalize(raw_latent, kv_gain):
    head_part = raw_latent[:, :KVL]
    inverse = lax.rsqrt(jnp.mean(head_part * head_part, axis=1, keepdims=True) + EPSILON)
    return jnp.concatenate(
        [head_part * inverse * kv_gain[None, :], raw_latent[:, KVL:]], axis=1
    ).astype(jnp.bfloat16)


def served_order(give_ref):
    first, second = give_ref[0], give_ref[1]
    low, high = jnp.minimum(first, second), jnp.maximum(first, second)
    kept_low = jnp.where(low > 0, 0, jnp.where(high > 1, 1, 2))
    kept_high = jnp.where(high < 3, 3, jnp.where(low < 2, 2, 1))
    return [first, second, kept_low, kept_high]


def resident_count(length):
    return (length + (PAGE - 1)) // PAGE - ARR


def across(a, b):
    return lax.dot_general(a, b, (((1,), (1,)), ((), ())), preferred_element_type=jnp.float32)


def pack_kernel(dest_ref, outbox_ref, out_ref, page_ref, stage_ref, index_ref, in_sems, out_sems):
    sent, groups = outbox_ref.shape[0], out_ref.shape[0]
    parts = in_sems.shape[0]
    step = sent // parts
    loads = [
        pltpu.make_async_copy(outbox_ref.at[pl.ds(i * step, step)], page_ref.at[pl.ds(i * step, step)], in_sems.at[i])
        for i in range(parts)
    ]
    for load in loads:
        load.start()
    page_ref[sent] = jnp.zeros_like(page_ref[sent])
    for i in range(groups * CAP):
        index_ref[i] = sent
    for i in range(sent):
        slot = dest_ref[i] * CAP
        index_ref[slot + (index_ref[slot] != sent).astype(jnp.int32)] = i
    for load in loads:
        load.wait()
    block = groups // out_sems.shape[0]
    stores = []
    for part in range(out_sems.shape[0]):
        for dest in range(part * block, (part + 1) * block):
            for rank in range(CAP):
                page = page_ref.at[index_ref[dest * CAP + rank]]
                stage_ref[dest, :, rank * KVL : (rank + 1) * KVL] = page[:, :KVL]
                stage_ref[dest, :, CAP * KVL + rank * ROPE : CAP * KVL + (rank + 1) * ROPE] = page[:, KVL:]
        span = pl.ds(part * block, block)
        store = pltpu.make_async_copy(stage_ref.at[span], out_ref.at[span], out_sems.at[part])
        store.start()
        stores.append(store)
    for store in stores:
        store.wait()


def resident_kernel(
    give_ref, table_ref, length_ref, cache_ref, query_ref, query_give, query_keep, blend_give, blend_keep, stat_ref, key_ref
):
    piece = cache_ref.shape[1]
    lane = lax.broadcasted_iota(jnp.int32, stat_ref.shape, 1)
    stats = jnp.zeros(stat_ref.shape, jnp.float32)
    for place, row in enumerate(served_order(give_ref)):
        count = resident_count(length_ref[row])
        for pair in range(RESMAX // 2):
            parts = []
            for half in range(2):
                entry = pair * 2 + half
                parts.append(cache_ref[table_ref[row, jnp.where(entry < count, entry, 0)]])
            key_ref[place, pair * 2 * piece : (pair + 1) * 2 * piece, :] = jnp.concatenate(parts, axis=0)
        query_t = query_ref[row].astype(jnp.float32)
        query = jnp.concatenate([query_t, query_t[KVL:]], axis=0).T.astype(jnp.bfloat16)
        queries, blends = (query_give, blend_give) if place < MOVES else (query_keep, blend_keep)
        queries[place % MOVES] = query
        keys = key_ref[place]
        scores = SCORE_SCALE * across(query[:, : KVL + ROPE], keys)
        token = lax.broadcasted_iota(jnp.int32, scores.shape, 1)
        scores = jnp.where(token < count * piece, scores, -jnp.inf)
        top = jnp.max(scores, axis=1, keepdims=True)
        weights = jnp.exp(scores - top)
        total = jnp.sum(weights, axis=1, keepdims=True)
        blends[place % MOVES] = jnp.dot(weights.astype(jnp.bfloat16), keys[:, :KVL], preferred_element_type=jnp.float32)
        stats = jnp.where(lane == place, top, jnp.where(lane == MAXROWS + place, total, stats))
    stat_ref[...] = stats


def own_kernel(latent_ref, query_give, query_keep, own_ref):
    lane = lax.broadcasted_iota(jnp.int32, own_ref.shape[1:], 1)
    latents = latent_ref[...]
    for part, queries in enumerate((query_give, query_keep)):
        own = jnp.zeros(own_ref.shape[1:], jnp.float32)
        for move in range(MOVES):
            place = part * MOVES + move
            scores = SCORE_SCALE * across(queries[move][:, : KVL + ROPE], latents)
            own = jnp.where(lane == move, scores[:, place : place + 1], own)
        own_ref[part] = own


def arrived_kernel(
    base, shard_ref, give_ref, table_ref, length_ref, arrived_ref, query_ref, blend_ref, stat_ref, send_ref
):
    shards, piece = send_ref.shape[0], arrived_ref.shape[1]
    rows, heads, _ = query_ref.shape
    own = heads // shards
    lane = lax.broadcasted_iota(jnp.int32, (heads, 128), 1)
    page_lane = lax.broadcasted_iota(jnp.int32, (piece, 128), 1)
    stats = jnp.zeros((heads, 128), jnp.float32)
    order = served_order(give_ref)
    keys, ropes = [], []
    for move in range(rows):
        row = order[base + move]
        count = resident_count(length_ref[row])
        latent_parts, rope_parts = [], []
        for entry in range(ARR):
            slot = table_ref[row, count + entry] - RES_POOL
            source, rank = slot // CAP, lax.rem(slot, CAP)
            latent_parts.append(arrived_ref[source, :, pl.ds(pl.multiple_of(rank * KVL, KVL), KVL)])
            both = arrived_ref[source, :, CAP * KVL : CAP * KVL + 128].astype(jnp.float32)
            rope_parts.append(jnp.where(page_lane // ROPE == rank, both, 0.0))
        keys.append(jnp.concatenate(latent_parts, axis=0))
        ropes.append(jnp.concatenate(rope_parts, axis=0).astype(jnp.bfloat16))
    for move in range(rows):
        row = order[base + move]
        length = length_ref[row]
        count = resident_count(length)
        query = query_ref[move]
        scores = SCORE_SCALE * (across(query[:, :KVL], keys[move]) + across(query[:, KVL:], ropes[move]))
        token = lax.broadcasted_iota(jnp.int32, scores.shape, 1)
        position = (count + token // piece) * PAGE + shard_ref[0] * piece + lax.rem(token, piece)
        scores = jnp.where(position < length, scores, -jnp.inf)
        old_top = stat_ref[:, base + move : base + move + 1]
        old_total = stat_ref[:, MAXROWS + base + move : MAXROWS + base + move + 1]
        top = jnp.maximum(jnp.max(scores, axis=1, keepdims=True), old_top)
        weights = jnp.exp(scores - top)
        shrink = jnp.exp(old_top - top)
        total = jnp.sum(weights, axis=1, keepdims=True) + shrink * old_total
        blend = jnp.dot(weights.astype(jnp.bfloat16), keys[move], preferred_element_type=jnp.float32)
        partial = ((blend + shrink * blend_ref[move]) * (1.0 / total)).astype(jnp.bfloat16)
        for shard_to in range(shards):
            for chunk in range(KVL // 128):
                start = (chunk * rows + move) * own
                send_ref[shard_to, start : start + own, :] = partial[
                    shard_to * own : (shard_to + 1) * own, chunk * 128 : (chunk + 1) * 128
                ]
        level = top + jnp.log(total)
        for piece_of in range(3):
            rounded = level.astype(jnp.bfloat16).astype(jnp.float32)
            stats = jnp.where(lane == piece_of * rows + move, rounded, stats)
            level = level - rounded
    coded = stats.astype(jnp.bfloat16)
    for shard_to in range(shards):
        send_ref[shard_to, KVL // 128 * rows * own :, :] = coded[shard_to * own : (shard_to + 1) * own]


def combined(base, shard_ref, received_ref, latent_ref, own_ref):
    shards = received_ref.shape[0]
    own = own_ref.shape[1] // shards
    stat_base = received_ref.shape[1] - own
    level_own = own_ref[base // MOVES, pl.ds(pl.multiple_of(shard_ref[0] * own, own), own), :]
    levels = []
    for share in range(shards):
        stats = received_ref[share, stat_base:, :].astype(jnp.float32)
        levels.append(stats + pltpu.roll(stats, 128 - MOVES, 1) + pltpu.roll(stats, 128 - 2 * MOVES, 1))
    peak = functools.reduce(jnp.maximum, levels, level_own)
    weights = [jnp.exp(level - peak) for level in levels] + [jnp.exp(level_own - peak)]
    inverse = 1.0 / functools.reduce(lambda a, b: a + b, weights)
    weights = [weight * inverse for weight in weights]
    results = []
    for move in range(MOVES):
        columns = [jnp.broadcast_to(weight[:, move : move + 1], weight.shape) for weight in weights]
        chunks = []
        for chunk in range(KVL // 128):
            value = columns[-1] * latent_ref[base + move : base + move + 1, chunk * 128 : (chunk + 1) * 128].astype(jnp.float32)
            start = (chunk * MOVES + move) * own
            for share in range(shards):
                value += columns[share] * received_ref[share, start : start + own, :].astype(jnp.float32)
            chunks.append(value.astype(jnp.bfloat16))
        results.append(jnp.concatenate(chunks, axis=1))
    return results


def give_kernel(shard_ref, received_ref, latent_ref, own_ref, out_ref):
    for move, result in enumerate(combined(0, shard_ref, received_ref, latent_ref, own_ref)):
        out_ref[move] = result


def keep_kernel(shard_ref, give_ref, received_ref, latent_ref, own_ref, taken_ref, out_ref):
    order = served_order(give_ref)
    for move, result in enumerate(combined(MOVES, shard_ref, received_ref, latent_ref, own_ref)):
        out_ref[order[MOVES + move]] = result
    for move in range(MOVES):
        out_ref[order[move]] = taken_ref[move]


def shards(
    hidden,
    kva_weight,
    kv_gain,
    queries,
    latent_cache,
    outbox,
    out_dest,
    page_table,
    lengths,
    give_rows,
):
    group_count = lax.axis_size("dp")
    shard_count = lax.axis_size("tp")
    shard = lax.axis_index("tp").astype(jnp.int32).reshape(1)
    row_count = hidden.shape[0]
    page_piece = latent_cache.shape[1]
    heads = queries.shape[1]
    own = heads // shard_count
    moves = give_rows.shape[0]
    query_t = jnp.swapaxes(queries, 1, 2)
    kept = row_count - moves
    wide = KVL + 2 * ROPE
    params = pltpu.CompilerParams(vmem_limit_bytes=VMEM_LIMIT)
    shape = jax.ShapeDtypeStruct

    outgoing = pl.pallas_call(
        pack_kernel,
        out_shape=shape((group_count, page_piece, CAP * (KVL + ROPE)), jnp.bfloat16),
        in_specs=[SMEM(), pl.BlockSpec(memory_space=pltpu.HBM)],
        out_specs=pl.BlockSpec(memory_space=pl.ANY),
        scratch_shapes=[
            pltpu.VMEM((outbox.shape[0] + 1,) + outbox.shape[1:], jnp.bfloat16),
            pltpu.VMEM((group_count, page_piece, CAP * (KVL + ROPE)), jnp.bfloat16),
            pltpu.SMEM((group_count * CAP,), jnp.int32),
            pltpu.SemaphoreType.DMA((8,)),
            pltpu.SemaphoreType.DMA((8,)),
        ],
        compiler_params=params,
        name="pack",
    )(out_dest, pltpu.with_memory_space_constraint(outbox, pltpu.HBM))
    arrived = lax.all_to_all(outgoing, "dp", split_axis=0, concat_axis=0, tiled=True)

    partial_raw = jnp.dot(hidden, kva_weight, preferred_element_type=jnp.float32)
    parts = lax.all_gather(partial_raw, "tp")
    home_latent = normalize(jnp.sum(parts, axis=0), kv_gain).astype(jnp.float32)
    partner = [(i, i ^ (group_count // 2)) for i in range(group_count)]
    row_ids = lax.broadcasted_iota(jnp.int32, (moves, row_count), 1)
    is_given = row_ids == give_rows[:, None]
    given = is_given[0] | is_given[1]
    kept_rank = jnp.cumsum(jnp.where(given, 0, 1)) - 1
    is_kept = jnp.logical_not(given)[None, :] & (kept_rank[None, :] == lax.broadcasted_iota(jnp.int32, (kept, row_count), 0))
    served = jnp.concatenate([is_given, is_kept, jnp.zeros((8 - row_count, row_count), jnp.bool_)], axis=0)
    latent = jnp.sum(jnp.where(served[:, :, None], home_latent[None], 0.0), axis=1).astype(jnp.bfloat16)
    moved_latent = lax.ppermute(latent[:moves], "dp", partner)
    new_latent = home_latent.astype(jnp.bfloat16)
    for move in range(moves):
        new_latent = jnp.where(is_given[move][:, None], moved_latent[move][None], new_latent)

    query_give, query_keep, blend_give, blend_keep, stats = pl.pallas_call(
        resident_kernel,
        out_shape=(
            shape((moves, heads, wide), jnp.bfloat16),
            shape((kept, heads, wide), jnp.bfloat16),
            shape((moves, heads, KVL), jnp.float32),
            shape((kept, heads, KVL), jnp.float32),
            shape((heads, 128), jnp.float32),
        ),
        in_specs=[SMEM(), SMEM(), SMEM(), VMEM(), VMEM()],
        out_specs=(VMEM(),) * 5,
        scratch_shapes=[pltpu.VMEM((row_count, RESMAX * page_piece, latent_cache.shape[2]), jnp.bfloat16)],
        compiler_params=params,
        name="resident",
    )(give_rows, page_table, lengths, latent_cache, query_t)
    own_scores = pl.pallas_call(
        own_kernel,
        out_shape=shape((2, heads, 128), jnp.float32),
        in_specs=[VMEM()] * 3,
        out_specs=VMEM(),
        compiler_params=params,
        name="own",
    )(latent, query_give, query_keep)

    def attend(base, query, blend, stats):
        return pl.pallas_call(
            functools.partial(arrived_kernel, base),
            out_shape=shape((shard_count, (KVL // 128 * moves + 1) * own, 128), jnp.bfloat16),
            in_specs=[SMEM()] * 4 + [VMEM()] * 4,
            out_specs=VMEM(),
            compiler_params=params,
            name="arrived",
        )(shard, give_rows, page_table, lengths, arrived, query, blend, stats)

    def swap(part):
        return lax.all_to_all(part, "tp", split_axis=0, concat_axis=0, tiled=True)

    send_give, stats = lax.optimization_barrier((attend(0, query_give, blend_give, stats), stats))
    received_give = swap(send_give)
    send_keep = attend(moves, query_keep, blend_keep, stats)
    handed = pl.pallas_call(
        give_kernel,
        out_shape=shape((moves, own, KVL), jnp.bfloat16),
        in_specs=[SMEM()] + [VMEM()] * 3,
        out_specs=VMEM(),
        compiler_params=params,
        name="give",
    )(shard, received_give, latent, own_scores)
    handed, send_keep = lax.optimization_barrier((handed, send_keep))
    taken = lax.ppermute(handed, "dp", partner)
    received_keep = swap(send_keep)
    attended = pl.pallas_call(
        keep_kernel,
        out_shape=shape((row_count, own, KVL), jnp.bfloat16),
        in_specs=[SMEM()] * 2 + [VMEM()] * 4,
        out_specs=VMEM(),
        compiler_params=params,
        name="keep",
    )(shard, give_rows, received_keep, latent, own_scores, taken)
    return (attended, new_latent)


def solution(mesh):
    placed = (
        P("dp", "tp"),
        P("tp", None),
        P(),
        P("dp", None, None),
        P("dp", "tp", None),
        P("dp", "tp", None),
        P("dp"),
        P("dp", None),
        P("dp"),
        P("dp"),
    )
    return jax.shard_map(
        shards,
        mesh=mesh,
        in_specs=placed,
        out_specs=(P("dp", "tp", None), P("dp", None)),
        check_vma=False,
    )
```

```python
import functools

import jax
import jax.numpy as jnp
from jax import lax
from jax.experimental import pallas as pl
from jax.experimental.pallas import tpu as pltpu
from jax.sharding import Mesh
from jax.sharding import PartitionSpec as P

KVL = 512
PAGE = 64
CAP = 2
ARR = 16
RESMAX = 24
MAXROWS = 4
MOVES = 2
ROPE = 64
RES_POOL = 96
SHARES = 8
DP, TP = ("half", "group"), ("x", "core")


EPSILON = 1e-06
SCORE_SCALE = 192.0 ** (-0.5)
VMEM_LIMIT = 32 * 1024 * 1024

SMEM = functools.partial(pl.BlockSpec, memory_space=pltpu.SMEM)
VMEM = functools.partial(pl.BlockSpec, memory_space=pltpu.VMEM)
HBM = functools.partial(pl.BlockSpec, memory_space=pltpu.HBM)
ANY = functools.partial(pl.BlockSpec, memory_space=pl.ANY)


def normalize(raw_latent, kv_gain):
    head_part = raw_latent[:, :KVL]
    inverse = lax.rsqrt(jnp.mean(head_part * head_part, axis=1, keepdims=True) + EPSILON)
    return jnp.concatenate(
        [head_part * inverse * kv_gain[None, :], raw_latent[:, KVL:]], axis=1
    )


def served_order(give_ref):
    first, second = give_ref[0], give_ref[1]
    low, high = jnp.minimum(first, second), jnp.maximum(first, second)
    kept_low = jnp.where(low > 0, 0, jnp.where(high > 1, 1, 2))
    kept_high = jnp.where(high < 3, 3, jnp.where(low < 2, 2, 1))
    return [first, second, kept_low, kept_high]


def resident_count(length):
    return (length + (PAGE - 1)) // PAGE - ARR


def across(a, b):
    return lax.dot_general(a, b, (((1,), (1,)), ((), ())), preferred_element_type=jnp.float32)


def pack_kernel(dest_hbm, outbox_ref, out_ref, page_ref, stage_ref, dest_ref, index_ref, in_sems, out_sems, dest_sem):
    sent, groups = outbox_ref.shape[0], out_ref.shape[0]
    parts = in_sems.shape[0]
    step = sent // parts
    dest_load = pltpu.make_async_copy(dest_hbm, dest_ref, dest_sem)
    dest_load.start()
    loads = [
        pltpu.make_async_copy(outbox_ref.at[pl.ds(i * step, step)], page_ref.at[pl.ds(i * step, step)], in_sems.at[i])
        for i in range(parts)
    ]
    for load in loads:
        load.start()
    page_ref[sent] = jnp.zeros_like(page_ref[sent])
    for i in range(groups * CAP):
        index_ref[i] = sent
    dest_load.wait()
    for i in range(sent):
        slot = dest_ref[i] * CAP
        index_ref[slot + (index_ref[slot] != sent).astype(jnp.int32)] = i
    for load in loads:
        load.wait()
    block = groups // out_sems.shape[0]
    stores = []
    for part in range(out_sems.shape[0]):
        for dest in range(part * block, (part + 1) * block):
            for rank in range(CAP):
                page = page_ref.at[index_ref[dest * CAP + rank]]
                stage_ref[dest, :, rank * KVL : (rank + 1) * KVL] = page[:, :KVL]
                stage_ref[dest, :, CAP * KVL + rank * ROPE : CAP * KVL + (rank + 1) * ROPE] = page[:, KVL:]
        span = pl.ds(part * block, block)
        store = pltpu.make_async_copy(stage_ref.at[span], out_ref.at[span], out_sems.at[part])
        store.start()
        stores.append(store)
    for store in stores:
        store.wait()


def resident_kernel(
    shard_ref, give_ref, table_ref, length_ref, cache_ref, query_ref, latent_ref, query_out, blend_out, stat_ref, key_ref
):
    piece = cache_ref.shape[1]
    heads = query_ref.shape[2]
    own = heads // SHARES
    shard = shard_ref[0]
    core = lax.rem(shard, 2)
    lane = lax.broadcasted_iota(jnp.int32, stat_ref.shape, 1)
    stats = jnp.zeros(stat_ref.shape, jnp.float32)
    order = served_order(give_ref)
    for place, row in enumerate(order):
        query_t = query_ref[row].astype(jnp.float32)
        query = jnp.concatenate([query_t, query_t[KVL:]], axis=0).T.astype(jnp.bfloat16)
        for device in range(SHARES):
            half = lax.rem(core + device, 2)
            start = pl.multiple_of(half * (heads // 2) + device // 2 * own, own)
            query_out[place, pl.ds(start, own), :] = query[device * own : (device + 1) * own]
        count = resident_count(length_ref[row])
        for pair in range(RESMAX // 2):
            parts = []
            for half in range(2):
                entry = pair * 2 + half
                parts.append(cache_ref[table_ref[row, jnp.where(entry < count, entry, 0)]])
            key_ref[place, pair * 2 * piece : (pair + 1) * 2 * piece, :] = jnp.concatenate(parts, axis=0)
    for place, row in enumerate(order):
        count = resident_count(length_ref[row])
        query = query_out[place][:, : KVL + ROPE]
        keys = key_ref[place]
        latent = latent_ref[pl.ds(row, 1), :]
        scores = SCORE_SCALE * across(query, keys)
        token = lax.broadcasted_iota(jnp.int32, scores.shape, 1)
        scores = jnp.where(token < count * piece, scores, -jnp.inf)
        fresh = SCORE_SCALE * jnp.sum(query.astype(jnp.float32) * latent, axis=1, keepdims=True)
        fresh = jnp.where(shard == 0, fresh, -jnp.inf)
        top = jnp.maximum(jnp.max(scores, axis=1, keepdims=True), fresh)
        weights = jnp.exp(scores - top)
        fresh_weight = jnp.exp(fresh - top)
        total = jnp.sum(weights, axis=1, keepdims=True) + fresh_weight
        blend = jnp.dot(weights.astype(jnp.bfloat16), keys[:, :KVL], preferred_element_type=jnp.float32)
        blend_out[place] = blend + fresh_weight * latent[:, :KVL]
        stats = jnp.where(lane == place, top, jnp.where(lane == MAXROWS + place, total, stats))
    stat_ref[...] = stats


def coded(level, lane, stride, place, stats):
    for term in range(3):
        rounded = level.astype(jnp.bfloat16).astype(jnp.float32)
        stats = jnp.where(lane == term * stride + place, rounded, stats)
        level = level - rounded
    return stats


def decoded(stats, stride):
    stats = stats.astype(jnp.float32)
    return stats + pltpu.roll(stats, 128 - stride, 1) + pltpu.roll(stats, 128 - 2 * stride, 1)


def arrived_kernel(
    shard_ref, give_ref, table_ref, length_ref, arrived_ref, query_ref, blend_hbm, stat_ref, mine_ref, other_ref, blend_ref, sems
):
    chips, piece = mine_ref.shape[0], arrived_ref.shape[1]
    rows, heads, _ = query_ref.shape
    own = heads // SHARES
    loads = [pltpu.make_async_copy(blend_hbm.at[place], blend_ref.at[place], sems.at[place]) for place in range(rows)]
    for load in loads:
        load.start()
    lane = lax.broadcasted_iota(jnp.int32, (heads, 128), 1)
    page_lane = lax.broadcasted_iota(jnp.int32, (piece, 128), 1)
    stats = jnp.zeros((heads, 128), jnp.float32)
    order = served_order(give_ref)
    keys, ropes = [], []
    for row in order:
        count = resident_count(length_ref[row])
        latent_parts, rope_parts = [], []
        for entry in range(ARR):
            slot = table_ref[row, count + entry] - RES_POOL
            source, rank = slot // CAP, lax.rem(slot, CAP)
            latent_parts.append(arrived_ref[source, :, pl.ds(pl.multiple_of(rank * KVL, KVL), KVL)])
            both = arrived_ref[source, :, CAP * KVL : CAP * KVL + 128].astype(jnp.float32)
            rope_parts.append(jnp.where(page_lane // ROPE == rank, both, 0.0))
        keys.append(jnp.concatenate(latent_parts, axis=0))
        ropes.append(jnp.concatenate(rope_parts, axis=0).astype(jnp.bfloat16))
    for place, row in enumerate(order):
        length = length_ref[row]
        count = resident_count(length)
        query = query_ref[place]
        scores = SCORE_SCALE * (across(query[:, :KVL], keys[place]) + across(query[:, KVL:], ropes[place]))
        token = lax.broadcasted_iota(jnp.int32, scores.shape, 1)
        position = (count + token // piece) * PAGE + shard_ref[0] * piece + lax.rem(token, piece)
        scores = jnp.where(position < length, scores, -jnp.inf)
        old_top = stat_ref[:, place : place + 1]
        old_total = stat_ref[:, MAXROWS + place : MAXROWS + place + 1]
        top = jnp.maximum(jnp.max(scores, axis=1, keepdims=True), old_top)
        weights = jnp.exp(scores - top)
        shrink = jnp.exp(old_top - top)
        total = jnp.sum(weights, axis=1, keepdims=True) + shrink * old_total
        blend = jnp.dot(weights.astype(jnp.bfloat16), keys[place], preferred_element_type=jnp.float32)
        loads[place].wait()
        partial = ((blend + shrink * blend_ref[place]) * (1.0 / total)).astype(jnp.bfloat16)
        for half, part_ref in enumerate((mine_ref, other_ref)):
            for chip in range(chips):
                first = (half * chips + chip) * own
                for chunk in range(KVL // 128):
                    start = (chunk * rows + place) * own
                    part_ref[chip, start : start + own, :] = partial[first : first + own, chunk * 128 : (chunk + 1) * 128]
        stats = coded(top + jnp.log(total), lane, rows, place, stats)
    stats = stats.astype(jnp.bfloat16)
    for half, part_ref in enumerate((mine_ref, other_ref)):
        for chip in range(chips):
            first = (half * chips + chip) * own
            part_ref[chip, KVL // 128 * rows * own :, :] = stats[first : first + own]


def merge_kernel(side_ref, mine_ref, other_ref, send_ref, stage_ref, sems):
    chips = mine_ref.shape[0]
    rows = MAXROWS
    own = mine_ref.shape[1] // (KVL // 128 * rows + 1)
    lane = lax.broadcasted_iota(jnp.int32, (own, 128), 1)
    side = side_ref[0]
    stat_base = KVL // 128 * rows * own
    stores = []
    for chip in range(chips):
        level_a = decoded(mine_ref[chip, stat_base:, :], rows)
        level_b = decoded(other_ref[chip, stat_base:, :], rows)
        peak = jnp.maximum(level_a, level_b)
        weight_a, weight_b = jnp.exp(level_a - peak), jnp.exp(level_b - peak)
        total = weight_a + weight_b
        level = peak + jnp.log(total)
        weight_a, weight_b = weight_a / total, weight_b / total
        for part in range(2):
            target = jnp.where(side == part, 1, 0) * chips + chip
            stats = jnp.zeros((own, 128), jnp.float32)
            for move in range(MOVES):
                place = part * MOVES + move
                column_a = jnp.broadcast_to(weight_a[:, place : place + 1], (own, 128))
                column_b = jnp.broadcast_to(weight_b[:, place : place + 1], (own, 128))
                for chunk in range(KVL // 128):
                    start = (chunk * rows + place) * own
                    value = column_a * mine_ref[chip, start : start + own, :].astype(jnp.float32)
                    value += column_b * other_ref[chip, start : start + own, :].astype(jnp.float32)
                    to = (chunk * MOVES + move) * own
                    stage_ref[target, to : to + own, :] = value.astype(jnp.bfloat16)
                stats = coded(level[:, place : place + 1], lane, MOVES, move, stats)
            stage_ref[target, KVL // 128 * MOVES * own :, :] = stats.astype(jnp.bfloat16)
            store = pltpu.make_async_copy(stage_ref.at[target], send_ref.at[target], sems.at[chip * 2 + part])
            store.start()
            stores.append(store)
    for store in stores:
        store.wait()


def finish_kernel(side_ref, give_ref, received_ref, out_ref):
    chips = received_ref.shape[0] // 2
    own = received_ref.shape[1] // (KVL // 128 * MOVES + 1)
    stat_base = KVL // 128 * MOVES * own
    order = served_order(give_ref)
    for part in range(2):
        base = jnp.where(side_ref[0] == part, 1, 0) * chips
        levels = [decoded(received_ref[base + chip, stat_base:, :], MOVES) for chip in range(chips)]
        peak = functools.reduce(jnp.maximum, levels)
        weights = [jnp.exp(level - peak) for level in levels]
        inverse = 1.0 / functools.reduce(lambda a, b: a + b, weights)
        weights = [weight * inverse for weight in weights]
        for move in range(MOVES):
            columns = [jnp.broadcast_to(weight[:, move : move + 1], weight.shape) for weight in weights]
            chunks = []
            for chunk in range(KVL // 128):
                start = (chunk * MOVES + move) * own
                value = columns[0] * received_ref[base, start : start + own, :].astype(jnp.float32)
                for chip in range(1, chips):
                    value += columns[chip] * received_ref[base + chip, start : start + own, :].astype(jnp.float32)
                chunks.append(value.astype(jnp.bfloat16))
            out_ref[order[part * MOVES + move]] = jnp.concatenate(chunks, axis=1)


def shards(
    hidden,
    kva_weight,
    kv_gain,
    queries,
    latent_cache,
    outbox,
    out_dest,
    page_table,
    lengths,
    give_rows,
):
    group_count = lax.axis_size(DP)
    chip_count = lax.axis_size("x")
    shard = lax.axis_index(TP).astype(jnp.int32).reshape(1)
    side = lax.axis_index("half").astype(jnp.int32).reshape(1)
    row_count = hidden.shape[0]
    page_piece = latent_cache.shape[1]
    heads = queries.shape[1]
    own = heads // SHARES
    moves = give_rows.shape[0]
    query_t = jnp.swapaxes(queries, 1, 2)
    wide = KVL + 2 * ROPE
    params = pltpu.CompilerParams(vmem_limit_bytes=VMEM_LIMIT)
    shape = jax.ShapeDtypeStruct
    in_hbm = functools.partial(pltpu.with_memory_space_constraint, memory_space=pltpu.HBM)

    outgoing = pl.pallas_call(
        pack_kernel,
        out_shape=shape((group_count, page_piece, CAP * (KVL + ROPE)), jnp.bfloat16),
        in_specs=[HBM(), HBM()],
        out_specs=ANY(),
        scratch_shapes=[
            pltpu.VMEM((outbox.shape[0] + 1,) + outbox.shape[1:], jnp.bfloat16),
            pltpu.VMEM((group_count, page_piece, CAP * (KVL + ROPE)), jnp.bfloat16),
            pltpu.SMEM(out_dest.shape, jnp.int32),
            pltpu.SMEM((group_count * CAP,), jnp.int32),
            pltpu.SemaphoreType.DMA((8,)),
            pltpu.SemaphoreType.DMA((8,)),
            pltpu.SemaphoreType.DMA,
        ],
        compiler_params=params,
        name="pack",
    )(in_hbm(out_dest), in_hbm(outbox))
    arrived = lax.all_to_all(outgoing, DP, split_axis=0, concat_axis=0, tiled=True)

    partial_raw = jnp.dot(hidden, kva_weight, preferred_element_type=jnp.float32)
    parts = lax.all_gather(partial_raw, TP)
    home_latent = lax.reduce_precision(normalize(jnp.sum(parts, axis=0), kv_gain), 8, 7)
    row_ids = lax.broadcasted_iota(jnp.int32, (moves, row_count), 1)
    is_given = row_ids == give_rows[:, None]
    handed_latent = jnp.sum(jnp.where(is_given[:, :, None], home_latent[None], 0.0), axis=1).astype(jnp.bfloat16)
    taken_latent = lax.ppermute(handed_latent, "half", [(0, 1), (1, 0)])
    new_latent = home_latent.astype(jnp.bfloat16)
    for move in range(moves):
        new_latent = jnp.where(is_given[move][:, None], taken_latent[move][None], new_latent)

    query, blend, stats = pl.pallas_call(
        resident_kernel,
        out_shape=(
            shape((row_count, heads, wide), jnp.bfloat16),
            shape((row_count, heads, KVL), jnp.float32),
            shape((heads, 128), jnp.float32),
        ),
        in_specs=[SMEM()] * 4 + [VMEM()] * 3,
        out_specs=(VMEM(),) * 3,
        scratch_shapes=[pltpu.VMEM((row_count, RESMAX * page_piece, latent_cache.shape[2]), jnp.bfloat16)],
        compiler_params=params,
        name="resident",
    )(shard, give_rows, page_table, lengths, latent_cache, query_t, home_latent)
    stats, new_latent = lax.optimization_barrier((stats, new_latent))

    part_shape = shape((chip_count, (KVL // 128 * row_count + 1) * own, 128), jnp.bfloat16)
    mine, other = pl.pallas_call(
        arrived_kernel,
        out_shape=(part_shape, part_shape),
        in_specs=[SMEM()] * 4 + [VMEM()] * 2 + [HBM(), VMEM()],
        out_specs=(VMEM(), VMEM()),
        scratch_shapes=[pltpu.VMEM((row_count, heads, KVL), jnp.float32), pltpu.SemaphoreType.DMA((row_count,))],
        compiler_params=params,
        name="arrived",
    )(shard, give_rows, page_table, lengths, arrived, query, in_hbm(blend), stats)
    other = lax.ppermute(other, "core", [(0, 1), (1, 0)])
    send_shape = (2 * chip_count, (KVL // 128 * moves + 1) * own, 128)
    outbound = pl.pallas_call(
        merge_kernel,
        out_shape=shape(send_shape, jnp.bfloat16),
        in_specs=[SMEM()] + [VMEM()] * 2,
        out_specs=ANY(),
        scratch_shapes=[pltpu.VMEM(send_shape, jnp.bfloat16), pltpu.SemaphoreType.DMA((2 * chip_count,))],
        compiler_params=params,
        name="merge",
    )(side, mine, other)
    received = lax.all_to_all(outbound, ("half", "x"), split_axis=0, concat_axis=0, tiled=True)
    attended = pl.pallas_call(
        finish_kernel,
        out_shape=shape((row_count, own, KVL), jnp.bfloat16),
        in_specs=[SMEM()] * 2 + [VMEM()],
        out_specs=VMEM(),
        compiler_params=params,
        name="finish",
    )(side, give_rows, received)
    return (attended, new_latent)


def solution(mesh):
    groups, shares = mesh.devices.shape
    split = Mesh(mesh.devices.reshape(2, groups // 2, shares // 2, 2), DP + TP)
    placed = (
        P(DP, TP),
        P(TP, None),
        P(),
        P(DP, None, None),
        P(DP, TP, None),
        P(DP, TP, None),
        P(DP),
        P(DP, None),
        P(DP),
        P(DP),
    )
    return jax.shard_map(
        shards,
        mesh=split,
        in_specs=placed,
        out_specs=(P(DP, TP, None), P(DP, None)),
        check_vma=False,
    )
```

```python
import functools

import jax
import jax.numpy as jnp
from jax import lax
from jax.experimental import pallas as pl
from jax.experimental.pallas import tpu as pltpu
from jax.sharding import Mesh
from jax.sharding import PartitionSpec as P

KVL = 512
PAGE = 64
CAP = 2
ARR = 16
RESMAX = 24
MAXROWS = 4
MOVES = 2
ROPE = 64
RES_POOL = 96
SHARES = 8
DP, TP = ("half", "group"), ("x", "core")
LATENT_ROWS = 5
META_SHARD, META_ROW, META_LEFT, META_SLOT = 0, 4, 8, 16


def interleaved(rank):
    y = (rank >> 5 & 1) * 4 + (rank >> 3 & 1) * 2 + (rank >> 1 & 1)
    z = (rank >> 4 & 1) * 4 + (rank >> 2 & 1) * 2 + (rank & 1)
    return y * 8 + z


ORDER = [interleaved(rank) for rank in range(64)]


EPSILON = 1e-06
SCORE_SCALE = 192.0 ** (-0.5)
VMEM_LIMIT = 32 * 1024 * 1024

SMEM = functools.partial(pl.BlockSpec, memory_space=pltpu.SMEM)
VMEM = functools.partial(pl.BlockSpec, memory_space=pltpu.VMEM)
HBM = functools.partial(pl.BlockSpec, memory_space=pltpu.HBM)
ANY = functools.partial(pl.BlockSpec, memory_space=pl.ANY)


def normalize(raw_latent, kv_gain):
    head_part = raw_latent[:, :KVL]
    inverse = lax.rsqrt(jnp.mean(head_part * head_part, axis=1, keepdims=True) + EPSILON)
    return jnp.concatenate(
        [head_part * inverse * kv_gain[None, :], raw_latent[:, KVL:]], axis=1
    )


def served_order(give_ref):
    first, second = give_ref[0], give_ref[1]
    low, high = jnp.minimum(first, second), jnp.maximum(first, second)
    kept_low = jnp.where(low > 0, 0, jnp.where(high > 1, 1, 2))
    kept_high = jnp.where(high < 3, 3, jnp.where(low < 2, 2, 1))
    return [first, second, kept_low, kept_high]


def resident_count(length):
    return (length + (PAGE - 1)) // PAGE - ARR


def stacked(rows, start=0, count=8):
    place = lax.broadcasted_iota(jnp.int32, (count, 128), 0)
    result = jnp.zeros((count, 128), jnp.float32)
    for index, row in enumerate(rows):
        result = jnp.where(place == start + index, row, result)
    return result


def turned(rows):
    return jnp.concatenate([rows, jnp.zeros((128 - rows.shape[0], 128), jnp.float32)], axis=0).T


def coded(level):
    terms = []
    for _ in range(3):
        terms.append(level.astype(jnp.bfloat16).astype(jnp.float32))
        level = level - terms[-1]
    return terms


def decoded(stats, count):
    stats = stats.astype(jnp.float32)
    return stats[:count] + stats[count : 2 * count] + stats[2 * count : 3 * count]


def blended(weights, values):
    return lax.dot_general(weights, values, (((0,), (0,)), ((), ())), preferred_element_type=jnp.float32)


def pack_kernel(dest_hbm, outbox_ref, out_ref, page_ref, stage_ref, dest_ref, index_ref, in_sems, out_sems, dest_sem):
    sent, groups = outbox_ref.shape[0], out_ref.shape[0]
    parts = in_sems.shape[0]
    step = sent // parts
    dest_load = pltpu.make_async_copy(dest_hbm, dest_ref, dest_sem)
    dest_load.start()
    loads = [
        pltpu.make_async_copy(outbox_ref.at[pl.ds(i * step, step)], page_ref.at[pl.ds(i * step, step)], in_sems.at[i])
        for i in range(parts)
    ]
    for load in loads:
        load.start()
    page_ref[sent] = jnp.zeros_like(page_ref[sent])
    for i in range(groups * CAP):
        index_ref[i] = sent
    dest_load.wait()
    for i in range(sent):
        slot = dest_ref[i] * CAP
        index_ref[slot + (index_ref[slot] != sent).astype(jnp.int32)] = i
    for load in loads:
        load.wait()
    block = groups // out_sems.shape[0]
    stores = []
    for part in range(out_sems.shape[0]):
        for dest in range(part * block, (part + 1) * block):
            for rank in range(CAP):
                page = page_ref.at[index_ref[ORDER[dest] * CAP + rank]]
                stage_ref[dest, :, rank * KVL : (rank + 1) * KVL] = page[:, :KVL]
                stage_ref[dest, :, CAP * KVL + rank * ROPE : CAP * KVL + (rank + 1) * ROPE] = page[:, KVL:]
        span = pl.ds(part * block, block)
        store = pltpu.make_async_copy(stage_ref.at[span], out_ref.at[span], out_sems.at[part])
        store.start()
        stores.append(store)
    for store in stores:
        store.wait()


def resident_kernel(
    shard_ref, give_ref, table_ref, length_ref, places_ref, cache_ref, query_ref, latent_ref,
    meta_ref, blend_out, stat_ref, handed_ref, key_ref,
):
    piece = cache_ref.shape[1]
    shard = shard_ref[0]
    resident = RESMAX * piece
    order = served_order(give_ref)
    tops, totals, handed = [], [], []
    meta_ref[META_SHARD] = shard
    for place, row in enumerate(order):
        length = length_ref[row]
        count = resident_count(length)
        meta_ref[META_ROW + place] = row
        meta_ref[META_LEFT + place] = length - count * PAGE
        for entry in range(ARR):
            slot = table_ref[row, count + entry] - RES_POOL
            meta_ref[META_SLOT + place * ARR + entry] = places_ref[slot // CAP] * CAP + lax.rem(slot, CAP)
        for pair in range(RESMAX // 2):
            parts = []
            for half in range(2):
                entry = pair * 2 + half
                parts.append(cache_ref[table_ref[row, jnp.where(entry < count, entry, 0)]])
            key_ref[place, pair * 2 * piece : (pair + 1) * 2 * piece, :] = jnp.concatenate(parts, axis=0)
        latent = latent_ref[pl.ds(row, 1), :]
        key_ref[place, resident:, :] = jnp.broadcast_to(latent, (16, latent.shape[1])).astype(jnp.bfloat16)
        if place < MOVES:
            latent = jnp.concatenate([latent, jnp.zeros((1, 128 - ROPE), jnp.float32)], axis=1)
            handed.extend(latent[:, chunk * 128 : (chunk + 1) * 128] for chunk in range(LATENT_ROWS))
    handed_ref[...] = stacked(handed, 3 * MOVES, 16)
    for place, row in enumerate(order):
        count = resident_count(length_ref[row])
        keys = key_ref[place]
        scores = SCORE_SCALE * jnp.dot(keys, query_ref[row], preferred_element_type=jnp.float32)
        token = lax.broadcasted_iota(jnp.int32, scores.shape, 0)
        fresh = jnp.where(shard == 0, resident, -1)
        scores = jnp.where((token < count * piece) | (token == fresh), scores, -jnp.inf)
        top = jnp.max(scores, axis=0, keepdims=True)
        weights = jnp.exp(scores - top)
        blend_out[place] = blended(weights.astype(jnp.bfloat16), keys[:, :KVL])
        tops.append(top)
        totals.append(jnp.sum(weights, axis=0, keepdims=True))
    stat_ref[...] = stacked(tops + totals)


def arrived_kernel(
    meta_ref, arrived_ref, query_hbm, blend_hbm, stat_ref, mine_ref, other_ref, query_ref, blend_ref, key_ref, rope_ref, sems
):
    piece = arrived_ref.shape[1]
    rows, _, heads = query_ref.shape
    own = heads // SHARES
    chips = SHARES // 2
    query_loads, blend_loads = [], []
    for place in range(rows):
        source = query_hbm.at[meta_ref[META_ROW + place]]
        query_loads.append(pltpu.make_async_copy(source, query_ref.at[place], sems.at[place]))
        query_loads[-1].start()
    for place in range(rows):
        blend_loads.append(pltpu.make_async_copy(blend_hbm.at[place], blend_ref.at[place], sems.at[rows + place]))
        blend_loads[-1].start()
    first_half = lax.broadcasted_iota(jnp.int32, (piece, 128), 1) // ROPE
    for place in range(rows):
        for pair in range(ARR // 2):
            latents, ropes = [], []
            for half in range(2):
                slot = meta_ref[META_SLOT + place * ARR + pair * 2 + half]
                source, rank = slot // CAP, lax.rem(slot, CAP)
                latents.append(arrived_ref[source, :, pl.ds(pl.multiple_of(rank * KVL, KVL), KVL)])
                both = arrived_ref[source, :, CAP * KVL : CAP * KVL + 128].astype(jnp.float32)
                ropes.append(jnp.where(first_half == rank, both, 0.0))
            span = slice(pair * 2 * piece, (pair + 1) * 2 * piece)
            key_ref[place, span, :] = jnp.concatenate(latents, axis=0)
            rope_ref[place, span, :] = jnp.concatenate(ropes, axis=0).astype(jnp.bfloat16)
    token = lax.broadcasted_iota(jnp.int32, (ARR * piece, heads), 0)
    position = token // piece * PAGE + meta_ref[META_SHARD] * piece + lax.rem(token, piece)
    levels, shrinks, weights = [], [], []
    for place in range(rows):
        query_loads[place].wait()
        query = query_ref[place]
        rope_query = jnp.concatenate([query[KVL:], query[KVL:]], axis=0)
        scores = jnp.dot(key_ref[place], query[:KVL], preferred_element_type=jnp.float32)
        scores += jnp.dot(rope_ref[place], rope_query, preferred_element_type=jnp.float32)
        scores = jnp.where(position < meta_ref[META_LEFT + place], SCORE_SCALE * scores, -jnp.inf)
        old_top, old_total = stat_ref[place : place + 1, :], stat_ref[MAXROWS + place : MAXROWS + place + 1, :]
        top = jnp.maximum(jnp.max(scores, axis=0, keepdims=True), old_top)
        shrink = jnp.exp(old_top - top)
        weight = jnp.exp(scores - top)
        total = jnp.sum(weight, axis=0, keepdims=True) + shrink * old_total
        inverse = 1.0 / total
        weights.append((weight * inverse).astype(jnp.bfloat16))
        shrinks.append(shrink * inverse)
        levels.append(top + jnp.log(total))
    columns = turned(stacked(shrinks))
    even = lax.rem(meta_ref[META_SHARD], 2) == 0
    for place in range(rows):
        blend = blended(weights[place], key_ref[place])
        blend_loads[place].wait()
        partial = (blend + columns[:, place : place + 1] * blend_ref[place]).astype(jnp.bfloat16)
        for chip in range(chips):
            block_even = partial[2 * chip * own : (2 * chip + 1) * own]
            block_odd = partial[(2 * chip + 1) * own : (2 * chip + 2) * own]
            block_mine = jnp.where(even, block_even, block_odd)
            block_other = jnp.where(even, block_odd, block_even)
            for chunk in range(KVL // 128):
                start = ((chip * (KVL // 128) + chunk) * rows + place) * own
                lanes = slice(chunk * 128, (chunk + 1) * 128)
                mine_ref[start : start + own, :] = block_mine[:, lanes]
                other_ref[start : start + own, :] = block_other[:, lanes]
    terms = coded(stacked(levels))
    stats = jnp.concatenate([terms[0][:rows], terms[1][:rows], terms[2][:rows], terms[0][rows:]], axis=0)
    stats = stats.astype(jnp.bfloat16)
    mine_ref[chips * (KVL // 128) * rows * own :, :] = stats
    other_ref[chips * (KVL // 128) * rows * own :, :] = stats


def merge_kernel(side_ref, meta_ref, mine_ref, other_ref, handed_ref, send_ref, column_ref):
    chips = SHARES // 2
    rows, own = MAXROWS, (mine_ref.shape[0] - 16) // (chips * (KVL // 128) * MAXROWS)
    side = side_ref[0]
    stat_base = chips * (KVL // 128) * rows * own
    level_a = decoded(mine_ref[stat_base:, :], rows)
    level_b = decoded(other_ref[stat_base:, :], rows)
    peak = jnp.maximum(level_a, level_b)
    weight_a, weight_b = jnp.exp(level_a - peak), jnp.exp(level_b - peak)
    total = weight_a + weight_b
    terms = coded(peak + jnp.log(total))
    inverse = 1.0 / total
    column_ref[...] = turned(jnp.concatenate([weight_a * inverse, weight_b * inverse], axis=0))
    core = lax.rem(meta_ref[META_SHARD], 2)
    stats = []
    for part in range(2):
        places = range(part * MOVES, (part + 1) * MOVES)
        kept = stacked([term[place : place + 1] for term in terms for place in places], 0, 16)
        stats.append((kept + handed_ref[...]).astype(jnp.bfloat16))
    for chip in range(chips):
        columns = column_ref[pl.ds(pl.multiple_of((2 * chip + core) * own, own), own), :]
        for part in range(2):
            target = jnp.where(side == part, 1, 0) * chips + chip
            for move in range(MOVES):
                place = part * MOVES + move
                column_a = jnp.broadcast_to(columns[:, place : place + 1], (own, 128))
                column_b = jnp.broadcast_to(columns[:, rows + place : rows + place + 1], (own, 128))
                for chunk in range(KVL // 128):
                    start = ((chip * (KVL // 128) + chunk) * rows + place) * own
                    value = column_a * mine_ref[start : start + own, :].astype(jnp.float32)
                    value += column_b * other_ref[start : start + own, :].astype(jnp.float32)
                    to = (chunk * MOVES + move) * own
                    send_ref[target, to : to + own, :] = value.astype(jnp.bfloat16)
            send_ref[target, KVL // 128 * MOVES * own :, :] = stats[part]


def finish_kernel(side_ref, meta_ref, received_ref, latent_ref, out_ref, latent_out, column_ref):
    chips = SHARES // 2
    own = out_ref.shape[1]
    stat_base = KVL // 128 * MOVES * own
    bases, weights = [], []
    for part in range(2):
        base = jnp.where(side_ref[0] == part, 1, 0) * chips
        bases.append(base)
        levels = [decoded(received_ref[base + chip, stat_base:, :], MOVES) for chip in range(chips)]
        peak = functools.reduce(jnp.maximum, levels)
        shares = [jnp.exp(level - peak) for level in levels]
        inverse = 1.0 / functools.reduce(lambda a, b: a + b, shares)
        weights.extend(share * inverse for share in shares)
    column_ref[...] = turned(jnp.concatenate(weights, axis=0))
    columns = column_ref[pl.ds(pl.multiple_of(meta_ref[META_SHARD] * own, own), own), :]
    for part in range(2):
        for move in range(MOVES):
            values = [0.0] * (KVL // 128)
            for chip in range(chips):
                lane = (part * chips + chip) * MOVES + move
                column = jnp.broadcast_to(columns[:, lane : lane + 1], (own, 128))
                for chunk in range(KVL // 128):
                    start = (chunk * MOVES + move) * own
                    block = received_ref[bases[part] + chip, start : start + own, :].astype(jnp.float32)
                    values[chunk] = values[chunk] + column * block
            row = meta_ref[META_ROW + part * MOVES + move]
            out_ref[row] = jnp.concatenate([value.astype(jnp.bfloat16) for value in values], axis=1)
    taken = received_ref[bases[0], stat_base:, :].astype(jnp.float32)
    latent = latent_ref[...]
    place = lax.broadcasted_iota(jnp.int32, latent.shape, 0)
    for move in range(MOVES):
        first = 3 * MOVES + move * LATENT_ROWS
        entry = jnp.concatenate([taken[first + chunk : first + chunk + 1] for chunk in range(LATENT_ROWS)], axis=1)
        latent = jnp.where(place == meta_ref[META_ROW + move], entry[:, : latent.shape[1]], latent)
    latent_out[...] = latent.astype(jnp.bfloat16)


def shards(
    hidden,
    kva_weight,
    kv_gain,
    queries,
    latent_cache,
    outbox,
    out_dest,
    page_table,
    lengths,
    give_rows,
):
    group_count = lax.axis_size(DP)
    chip_count = lax.axis_size("x")
    shard = lax.axis_index(TP).astype(jnp.int32).reshape(1)
    side = lax.axis_index("half").astype(jnp.int32).reshape(1)
    row_count = hidden.shape[0]
    page_piece = latent_cache.shape[1]
    heads = queries.shape[1]
    own = heads // SHARES
    moves = give_rows.shape[0]
    query_t = jnp.swapaxes(queries, 1, 2)
    params = pltpu.CompilerParams(vmem_limit_bytes=VMEM_LIMIT)
    shape = jax.ShapeDtypeStruct
    in_hbm = functools.partial(pltpu.with_memory_space_constraint, memory_space=pltpu.HBM)

    outgoing = pl.pallas_call(
        pack_kernel,
        out_shape=shape((group_count, page_piece, CAP * (KVL + ROPE)), jnp.bfloat16),
        in_specs=[HBM(), HBM()],
        out_specs=ANY(),
        scratch_shapes=[
            pltpu.VMEM((outbox.shape[0] + 1,) + outbox.shape[1:], jnp.bfloat16),
            pltpu.VMEM((group_count, page_piece, CAP * (KVL + ROPE)), jnp.bfloat16),
            pltpu.SMEM(out_dest.shape, jnp.int32),
            pltpu.SMEM((group_count * CAP,), jnp.int32),
            pltpu.SemaphoreType.DMA((8,)),
            pltpu.SemaphoreType.DMA((8,)),
            pltpu.SemaphoreType.DMA,
        ],
        compiler_params=params,
        name="pack",
    )(in_hbm(out_dest), in_hbm(outbox))
    arrived = lax.all_to_all(outgoing, DP, split_axis=0, concat_axis=0, tiled=True, axis_index_groups=[ORDER])

    partial_raw = jnp.dot(hidden, kva_weight, preferred_element_type=jnp.float32)
    parts = lax.all_gather(partial_raw, TP)
    latent = lax.reduce_precision(normalize(jnp.sum(parts, axis=0), kv_gain), 8, 7)

    places = [0] * group_count
    for place, group in enumerate(ORDER):
        places[group] = place
    meta, blend, stats, handed = pl.pallas_call(
        resident_kernel,
        out_shape=(
            shape((128,), jnp.int32),
            shape((row_count, heads, KVL), jnp.float32),
            shape((2 * MAXROWS, heads), jnp.float32),
            shape((16, 128), jnp.float32),
        ),
        in_specs=[SMEM()] * 5 + [VMEM()] * 3,
        out_specs=(SMEM(),) + (VMEM(),) * 3,
        scratch_shapes=[pltpu.VMEM((row_count, RESMAX * page_piece + 16, latent_cache.shape[2]), jnp.bfloat16)],
        compiler_params=params,
        name="resident",
    )(shard, give_rows, page_table, lengths, jnp.array(places, jnp.int32), latent_cache, query_t, latent)

    part_shape = shape((chip_count * (KVL // 128) * row_count * own + 16, 128), jnp.bfloat16)
    mine, other = pl.pallas_call(
        arrived_kernel,
        out_shape=(part_shape, part_shape),
        in_specs=[SMEM(), VMEM(), HBM(), HBM(), VMEM()],
        out_specs=(VMEM(), VMEM()),
        scratch_shapes=[
            pltpu.VMEM(query_t.shape, jnp.bfloat16),
            pltpu.VMEM((row_count, heads, KVL), jnp.float32),
            pltpu.VMEM((row_count, ARR * page_piece, KVL), jnp.bfloat16),
            pltpu.VMEM((row_count, ARR * page_piece, 128), jnp.bfloat16),
            pltpu.SemaphoreType.DMA((2 * row_count,)),
        ],
        compiler_params=params,
        name="arrived",
    )(meta, arrived, in_hbm(query_t), in_hbm(blend), stats)
    other = lax.ppermute(other, "core", [(0, 1), (1, 0)])
    outbound = pl.pallas_call(
        merge_kernel,
        out_shape=shape((2 * chip_count, KVL // 128 * moves * own + 16, 128), jnp.bfloat16),
        in_specs=[SMEM()] * 2 + [VMEM()] * 3,
        out_specs=VMEM(),
        scratch_shapes=[pltpu.VMEM((heads, 128), jnp.float32)],
        compiler_params=params,
        name="merge",
    )(side, meta, mine, other, handed)
    received = lax.all_to_all(outbound, ("half", "x"), split_axis=0, concat_axis=0, tiled=True)
    return pl.pallas_call(
        finish_kernel,
        out_shape=(
            shape((row_count, own, KVL), jnp.bfloat16),
            shape(latent.shape, jnp.bfloat16),
        ),
        in_specs=[SMEM()] * 2 + [VMEM()] * 2,
        out_specs=(VMEM(), VMEM()),
        scratch_shapes=[pltpu.VMEM((heads, 128), jnp.float32)],
        compiler_params=params,
        name="finish",
    )(side, meta, received, latent)


def solution(mesh):
    groups, shares = mesh.devices.shape
    split = Mesh(mesh.devices.reshape(2, groups // 2, shares // 2, 2), DP + TP)
    placed = (
        P(DP, TP),
        P(TP, None),
        P(),
        P(DP, None, None),
        P(DP, TP, None),
        P(DP, TP, None),
        P(DP),
        P(DP, None),
        P(DP),
        P(DP),
    )
    return jax.shard_map(
        shards,
        mesh=split,
        in_specs=placed,
        out_specs=(P(DP, TP, None), P(DP, None)),
        check_vma=False,
    )
```

```python
import functools

import jax
import jax.numpy as jnp
from jax import lax
from jax.experimental import pallas as pl
from jax.experimental.pallas import tpu as pltpu
from jax.sharding import Mesh
from jax.sharding import PartitionSpec as P

KVL = 512
PAGE = 64
CAP = 2
ARR = 16
RESMAX = 24
MAXROWS = 4
MOVES = 2
ROPE = 64
RES_POOL = 96
SHARES = 8
DP, TP = ("half", "group"), ("x", "core")
LATENT_ROWS = 5
META_LEFT, META_SLOT = 8, 16


ORDER = [y * 8 + z for y in range(7, -1, -1) for z in (7, 6, 5, 4, 0, 1, 2, 3)]


EPSILON = 1e-06
SCORE_SCALE = 192.0 ** (-0.5)
VMEM_LIMIT = 32 * 1024 * 1024

SMEM = functools.partial(pl.BlockSpec, memory_space=pltpu.SMEM)
VMEM = functools.partial(pl.BlockSpec, memory_space=pltpu.VMEM)
HBM = functools.partial(pl.BlockSpec, memory_space=pltpu.HBM)
ANY = functools.partial(pl.BlockSpec, memory_space=pl.ANY)


def normalize(raw_latent, kv_gain):
    head_part = raw_latent[:, :KVL]
    inverse = lax.rsqrt(jnp.mean(head_part * head_part, axis=1, keepdims=True) + EPSILON)
    return jnp.concatenate(
        [head_part * inverse * kv_gain[None, :], raw_latent[:, KVL:]], axis=1
    )


def served_order(give_ref):
    first, second = give_ref[0], give_ref[1]
    low, high = jnp.minimum(first, second), jnp.maximum(first, second)
    kept_low = jnp.where(low > 0, 0, jnp.where(high > 1, 1, 2))
    kept_high = jnp.where(high < 3, 3, jnp.where(low < 2, 2, 1))
    return [first, second, kept_low, kept_high]


def share_index():
    return lax.axis_index("x") * 2 + lax.axis_index("core")


def resident_count(length):
    return (length + (PAGE - 1)) // PAGE - ARR


def stacked(rows, start=0, count=8):
    place = lax.broadcasted_iota(jnp.int32, (count, 128), 0)
    result = jnp.zeros((count, 128), jnp.float32)
    for index, row in enumerate(rows):
        result = jnp.where(place == start + index, row, result)
    return result


def turned(rows):
    return jnp.concatenate([rows, jnp.zeros((128 - rows.shape[0], 128), jnp.float32)], axis=0).T


def coded(level):
    terms = []
    for _ in range(3):
        terms.append(level.astype(jnp.bfloat16).astype(jnp.float32))
        level = level - terms[-1]
    return terms


def decoded(stats, count):
    stats = stats.astype(jnp.float32)
    return stats[:count] + stats[count : 2 * count] + stats[2 * count : 3 * count]


def blended(weights, values):
    return lax.dot_general(weights, values, (((0,), (0,)), ((), ())), preferred_element_type=jnp.float32)


def pack_kernel(dest_hbm, outbox_ref, out_ref, page_ref, stage_ref, dest_ref, index_ref, in_sems, out_sems, dest_sem):
    sent, groups = outbox_ref.shape[0], out_ref.shape[0]
    parts = in_sems.shape[0]
    step = sent // parts
    dest_load = pltpu.make_async_copy(dest_hbm, dest_ref, dest_sem)
    dest_load.start()
    loads = [
        pltpu.make_async_copy(outbox_ref.at[pl.ds(i * step, step)], page_ref.at[pl.ds(i * step, step)], in_sems.at[i])
        for i in range(parts)
    ]
    for load in loads:
        load.start()
    page_ref[sent] = jnp.zeros_like(page_ref[sent])
    for i in range(groups * CAP):
        index_ref[i] = sent
    dest_load.wait()
    for i in range(sent):
        slot = dest_ref[i] * CAP
        index_ref[slot + (index_ref[slot] != sent).astype(jnp.int32)] = i
    for load in loads:
        load.wait()
    block = groups // out_sems.shape[0]
    stores = []
    for part in range(out_sems.shape[0]):
        for dest in range(part * block, (part + 1) * block):
            for rank in range(CAP):
                page = page_ref.at[index_ref[ORDER[dest] * CAP + rank]]
                stage_ref[dest, :, rank * KVL : (rank + 1) * KVL] = page[:, :KVL]
                stage_ref[dest, :, CAP * KVL + rank * ROPE : CAP * KVL + (rank + 1) * ROPE] = page[:, KVL:]
        span = pl.ds(part * block, block)
        store = pltpu.make_async_copy(stage_ref.at[span], out_ref.at[span], out_sems.at[part])
        store.start()
        stores.append(store)
    for store in stores:
        store.wait()


def resident_kernel(
    give_ref, table_ref, length_ref, places_ref, cache_ref, query_ref, latent_ref, meta_ref, stat_ref, handed_ref, place_ref, *refs
):
    query_outs, blend_out, key_ref = refs[:-2], refs[-2], refs[-1]
    piece = cache_ref.shape[1]
    shard = share_index()
    resident = RESMAX * piece
    order = served_order(give_ref)
    tops, totals, handed = [], [], []
    row_ids = lax.broadcasted_iota(jnp.int32, place_ref.shape, 0)
    places = jnp.zeros(place_ref.shape, jnp.int32)
    for place, row in enumerate(order):
        places = jnp.where(row_ids == row, place, places)
        query_outs[0][place] = query_ref[row]
        length = length_ref[row]
        count = resident_count(length)
        meta_ref[META_LEFT + place] = length - count * PAGE
        for entry in range(ARR):
            slot = table_ref[row, count + entry] - RES_POOL
            meta_ref[META_SLOT + place * ARR + entry] = places_ref[slot // CAP] * CAP + lax.rem(slot, CAP)
        for pair in range(RESMAX // 2):
            parts = []
            for half in range(2):
                entry = pair * 2 + half
                parts.append(cache_ref[table_ref[row, jnp.where(entry < count, entry, 0)]])
            key_ref[place, pair * 2 * piece : (pair + 1) * 2 * piece, :] = jnp.concatenate(parts, axis=0)
        latent = latent_ref[pl.ds(row, 1), :]
        key_ref[place, resident:, :] = jnp.broadcast_to(latent, (16, latent.shape[1])).astype(jnp.bfloat16)
        if place < MOVES:
            latent = jnp.concatenate([latent, jnp.zeros((1, 128 - ROPE), jnp.float32)], axis=1)
            handed.extend(latent[:, chunk * 128 : (chunk + 1) * 128] for chunk in range(LATENT_ROWS))
    handed_ref[...] = stacked(handed, 3 * MOVES, 16)
    place_ref[...] = places
    for place, row in enumerate(order):
        count = resident_count(length_ref[row])
        keys = key_ref[place]
        scores = SCORE_SCALE * jnp.dot(keys, query_outs[0][place], preferred_element_type=jnp.float32)
        token = lax.broadcasted_iota(jnp.int32, scores.shape, 0)
        fresh = jnp.where(shard == 0, resident, -1)
        scores = jnp.where((token < count * piece) | (token == fresh), scores, -jnp.inf)
        top = jnp.max(scores, axis=0, keepdims=True)
        weights = jnp.exp(scores - top)
        blend_out[place] = blended(weights.astype(jnp.bfloat16), keys[:, :KVL])
        tops.append(top)
        totals.append(jnp.sum(weights, axis=0, keepdims=True))
    stat_ref[...] = stacked(tops + totals)


def arrived_kernel(meta_hbm, blend_hbm, query_hbm, arrived_ref, stat_ref, *refs):
    mine_ref, other_ref, key_ref, rope_ref, blend_refs, query_refs, meta_ref, sems = refs
    loads = [pltpu.make_async_copy(meta_hbm, meta_ref, sems.at[MAXROWS])]
    query_loads = [pltpu.make_async_copy(query_hbm.at[place], query_refs.at[place], sems.at[MAXROWS + 1 + place]) for place in range(MAXROWS)]
    loads += [pltpu.make_async_copy(blend_hbm.at[place], blend_refs.at[place], sems.at[place]) for place in range(MAXROWS)]
    for load in loads[:1] + query_loads + loads[1:]:
        load.start()
    loads[0].wait()
    piece = arrived_ref.shape[1]
    rows, heads = MAXROWS, stat_ref.shape[1]
    own = heads // SHARES
    chips = SHARES // 2
    first_half = lax.broadcasted_iota(jnp.int32, (piece, 128), 1) // ROPE
    for place in range(rows):
        for pair in range(ARR // 2):
            latents, ropes = [], []
            for half in range(2):
                slot = meta_ref[META_SLOT + place * ARR + pair * 2 + half]
                source, rank = slot // CAP, lax.rem(slot, CAP)
                latents.append(arrived_ref[source, :, pl.ds(pl.multiple_of(rank * KVL, KVL), KVL)])
                both = arrived_ref[source, :, CAP * KVL : CAP * KVL + 128].astype(jnp.float32)
                ropes.append(jnp.where(first_half == rank, both, 0.0))
            span = slice(pair * 2 * piece, (pair + 1) * 2 * piece)
            key_ref[place, span, :] = jnp.concatenate(latents, axis=0)
            rope_ref[place, span, :] = jnp.concatenate(ropes, axis=0).astype(jnp.bfloat16)
    token = lax.broadcasted_iota(jnp.int32, (ARR * piece, heads), 0)
    position = token // piece * PAGE + share_index() * piece + lax.rem(token, piece)
    levels, shrinks, weights = [], [], []
    for load in query_loads:
        load.wait()
    for place in range(rows):
        query = query_refs[place]
        rope_query = jnp.concatenate([query[KVL:], query[KVL:]], axis=0)
        scores = jnp.dot(key_ref[place], query[:KVL], preferred_element_type=jnp.float32)
        scores += jnp.dot(rope_ref[place], rope_query, preferred_element_type=jnp.float32)
        scores = jnp.where(position < meta_ref[META_LEFT + place], SCORE_SCALE * scores, -jnp.inf)
        old_top, old_total = stat_ref[place : place + 1, :], stat_ref[MAXROWS + place : MAXROWS + place + 1, :]
        top = jnp.maximum(jnp.max(scores, axis=0, keepdims=True), old_top)
        shrink = jnp.exp(old_top - top)
        weight = jnp.exp(scores - top)
        total = jnp.sum(weight, axis=0, keepdims=True) + shrink * old_total
        inverse = 1.0 / total
        weights.append((weight * inverse).astype(jnp.bfloat16))
        shrinks.append(shrink * inverse)
        levels.append(top + jnp.log(total))
    columns = turned(stacked(shrinks))
    for load in loads[1:]:
        load.wait()
    even = lax.axis_index("core") == 0
    for place in range(rows):
        blend = blended(weights[place], key_ref[place])
        partial = (blend + columns[:, place : place + 1] * blend_refs[place]).astype(jnp.bfloat16)
        for chip in range(chips):
            block_even = partial[2 * chip * own : (2 * chip + 1) * own]
            block_odd = partial[(2 * chip + 1) * own : (2 * chip + 2) * own]
            block_mine = jnp.where(even, block_even, block_odd)
            block_other = jnp.where(even, block_odd, block_even)
            for chunk in range(KVL // 128):
                start = ((chip * (KVL // 128) + chunk) * rows + place) * own
                lanes = slice(chunk * 128, (chunk + 1) * 128)
                mine_ref[start : start + own, :] = block_mine[:, lanes]
                other_ref[start : start + own, :] = block_other[:, lanes]
    terms = coded(stacked(levels))
    stats = jnp.concatenate([terms[0][:rows], terms[1][:rows], terms[2][:rows], terms[0][rows:]], axis=0)
    stats = stats.astype(jnp.bfloat16)
    mine_ref[chips * (KVL // 128) * rows * own :, :] = stats
    other_ref[chips * (KVL // 128) * rows * own :, :] = stats


def merge_kernel(mine_ref, other_ref, handed_ref, send_ref, column_ref):
    chips = SHARES // 2
    rows, own = MAXROWS, (mine_ref.shape[0] - 16) // (chips * (KVL // 128) * MAXROWS)
    side = lax.axis_index("half")
    stat_base = chips * (KVL // 128) * rows * own
    level_a = decoded(mine_ref[stat_base:, :], rows)
    level_b = decoded(other_ref[stat_base:, :], rows)
    peak = jnp.maximum(level_a, level_b)
    weight_a, weight_b = jnp.exp(level_a - peak), jnp.exp(level_b - peak)
    total = weight_a + weight_b
    terms = coded(peak + jnp.log(total))
    inverse = 1.0 / total
    column_ref[...] = turned(jnp.concatenate([weight_a * inverse, weight_b * inverse], axis=0))
    core = lax.axis_index("core")
    stats = []
    for part in range(2):
        places = range(part * MOVES, (part + 1) * MOVES)
        kept = stacked([term[place : place + 1] for term in terms for place in places], 0, 16)
        stats.append((kept + handed_ref[...]).astype(jnp.bfloat16))
    for chip in range(chips):
        columns = column_ref[pl.ds(pl.multiple_of((2 * chip + core) * own, own), own), :]
        for part in range(2):
            target = jnp.where(side == part, 1, 0) * chips + chip
            for move in range(MOVES):
                place = part * MOVES + move
                column_a = jnp.broadcast_to(columns[:, place : place + 1], (own, 128))
                column_b = jnp.broadcast_to(columns[:, rows + place : rows + place + 1], (own, 128))
                for chunk in range(KVL // 128):
                    start = ((chip * (KVL // 128) + chunk) * rows + place) * own
                    value = column_a * mine_ref[start : start + own, :].astype(jnp.float32)
                    value += column_b * other_ref[start : start + own, :].astype(jnp.float32)
                    to = (chunk * MOVES + move) * own
                    send_ref[target, to : to + own, :] = value.astype(jnp.bfloat16)
            send_ref[target, KVL // 128 * MOVES * own :, :] = stats[part]


def finish_kernel(received_ref, latent_ref, place_ref, out_ref, latent_out, column_ref):
    chips = SHARES // 2
    own = out_ref.shape[1]
    stat_base = KVL // 128 * MOVES * own
    bases, weights = [], []
    for part in range(2):
        base = jnp.where(lax.axis_index("half") == part, 1, 0) * chips
        bases.append(base)
        levels = [decoded(received_ref[base + chip, stat_base:, :], MOVES) for chip in range(chips)]
        peak = functools.reduce(jnp.maximum, levels)
        shares = [jnp.exp(level - peak) for level in levels]
        inverse = 1.0 / functools.reduce(lambda a, b: a + b, shares)
        weights.extend(share * inverse for share in shares)
    column_ref[...] = turned(jnp.concatenate(weights, axis=0))
    columns = column_ref[pl.ds(pl.multiple_of(share_index() * own, own), own), :]
    results = []
    for part in range(2):
        for move in range(MOVES):
            values = [0.0] * (KVL // 128)
            for chip in range(chips):
                lane = (part * chips + chip) * MOVES + move
                column = jnp.broadcast_to(columns[:, lane : lane + 1], (own, 128))
                for chunk in range(KVL // 128):
                    start = (chunk * MOVES + move) * own
                    block = received_ref[bases[part] + chip, start : start + own, :].astype(jnp.float32)
                    values[chunk] = values[chunk] + column * block
            results.append(values)
    for row in range(MAXROWS):
        at = jnp.broadcast_to(place_ref[row : row + 1, :], (own, 128))
        for chunk in range(KVL // 128):
            value = results[MAXROWS - 1][chunk]
            for place in range(MAXROWS - 1):
                value = jnp.where(at == place, results[place][chunk], value)
            out_ref[row, :, chunk * 128 : (chunk + 1) * 128] = value.astype(jnp.bfloat16)
    taken = received_ref[bases[0], stat_base:, :].astype(jnp.float32)
    latent = latent_ref[...]
    rows, width = latent.shape
    at = jnp.concatenate([place_ref[:rows, :]] * LATENT_ROWS, axis=1)[:, :width]
    for move in range(MOVES):
        first = 3 * MOVES + move * LATENT_ROWS
        entry = jnp.concatenate([taken[first + chunk : first + chunk + 1] for chunk in range(LATENT_ROWS)], axis=1)
        latent = jnp.where(at == move, entry[:, :width], latent)
    latent_out[...] = latent.astype(jnp.bfloat16)


def shards(
    hidden,
    kva_weight,
    kv_gain,
    queries,
    latent_cache,
    outbox,
    out_dest,
    page_table,
    lengths,
    give_rows,
):
    group_count = lax.axis_size(DP)
    chip_count = lax.axis_size("x")
    row_count = hidden.shape[0]
    page_piece = latent_cache.shape[1]
    heads = queries.shape[1]
    own = heads // SHARES
    moves = give_rows.shape[0]
    query_t = jnp.swapaxes(queries, 1, 2)
    params = pltpu.CompilerParams(vmem_limit_bytes=VMEM_LIMIT)
    shape = jax.ShapeDtypeStruct
    in_hbm = functools.partial(pltpu.with_memory_space_constraint, memory_space=pltpu.HBM)

    outgoing = pl.pallas_call(
        pack_kernel,
        out_shape=shape((group_count, page_piece, CAP * (KVL + ROPE)), jnp.bfloat16),
        in_specs=[HBM(), HBM()],
        out_specs=ANY(),
        scratch_shapes=[
            pltpu.VMEM((outbox.shape[0] + 1,) + outbox.shape[1:], jnp.bfloat16),
            pltpu.VMEM((group_count, page_piece, CAP * (KVL + ROPE)), jnp.bfloat16),
            pltpu.SMEM(out_dest.shape, jnp.int32),
            pltpu.SMEM((group_count * CAP,), jnp.int32),
            pltpu.SemaphoreType.DMA((8,)),
            pltpu.SemaphoreType.DMA((8,)),
            pltpu.SemaphoreType.DMA,
        ],
        compiler_params=params,
        name="pack",
    )(in_hbm(out_dest), in_hbm(outbox))
    arrived = lax.all_to_all(outgoing, DP, split_axis=0, concat_axis=0, tiled=True, axis_index_groups=[ORDER])

    partial_raw = jnp.dot(hidden, kva_weight, preferred_element_type=jnp.float32)
    parts = lax.all_gather(partial_raw, TP)
    latent = lax.reduce_precision(normalize(jnp.sum(parts, axis=0), kv_gain), 8, 7)

    places = [0] * group_count
    for place, group in enumerate(ORDER):
        places[group] = place
    meta, stats, handed, place, *operands, blend = pl.pallas_call(
        resident_kernel,
        out_shape=(
            shape((128,), jnp.int32),
            shape((2 * MAXROWS, heads), jnp.float32),
            shape((16, 128), jnp.float32),
            shape((8, 128), jnp.int32),
        )
        + (shape(query_t.shape, jnp.bfloat16),)
        + (shape((row_count, heads, KVL), jnp.float32),),
        in_specs=[SMEM()] * 4 + [VMEM()] * 3,
        out_specs=(SMEM(),) + (VMEM(),) * 5,
        scratch_shapes=[pltpu.VMEM((row_count, RESMAX * page_piece + 16, latent_cache.shape[2]), jnp.bfloat16)],
        compiler_params=params,
        name="resident",
    )(give_rows, page_table, lengths, jnp.array(places, jnp.int32), latent_cache, query_t, latent)

    part_shape = shape((chip_count * (KVL // 128) * row_count * own + 16, 128), jnp.bfloat16)
    mine, other = pl.pallas_call(
        arrived_kernel,
        out_shape=(part_shape, part_shape),
        in_specs=[HBM()] * 3 + [VMEM()] * 2,
        out_specs=(VMEM(), VMEM()),
        scratch_shapes=[
            pltpu.VMEM((row_count, ARR * page_piece, KVL), jnp.bfloat16),
            pltpu.VMEM((row_count, ARR * page_piece, 128), jnp.bfloat16),
            pltpu.VMEM((row_count, heads, KVL), jnp.float32),
            pltpu.VMEM(query_t.shape, jnp.bfloat16),
            pltpu.SMEM((128,), jnp.int32),
            pltpu.SemaphoreType.DMA((2 * row_count + 1,)),
        ],
        compiler_params=params,
        name="arrived",
    )(in_hbm(meta), in_hbm(blend), in_hbm(operands[0]), arrived, stats)
    other = lax.ppermute(other, "core", [(0, 1), (1, 0)])
    outbound = pl.pallas_call(
        merge_kernel,
        out_shape=shape((2 * chip_count, KVL // 128 * moves * own + 16, 128), jnp.bfloat16),
        in_specs=[VMEM()] * 3,
        out_specs=VMEM(),
        scratch_shapes=[pltpu.VMEM((heads, 128), jnp.float32)],
        compiler_params=params,
        name="merge",
    )(mine, other, handed)
    received = lax.all_to_all(outbound, ("half", "x"), split_axis=0, concat_axis=0, tiled=True)
    return pl.pallas_call(
        finish_kernel,
        out_shape=(
            shape((row_count, own, KVL), jnp.bfloat16),
            shape(latent.shape, jnp.bfloat16),
        ),
        in_specs=[VMEM()] * 3,
        out_specs=(VMEM(), VMEM()),
        scratch_shapes=[pltpu.VMEM((heads, 128), jnp.float32)],
        compiler_params=params,
        name="finish",
    )(received, latent, place)


def solution(mesh):
    groups, shares = mesh.devices.shape
    split = Mesh(mesh.devices.reshape(2, groups // 2, shares // 2, 2), DP + TP)
    placed = (
        P(DP, TP),
        P(TP, None),
        P(),
        P(DP, None, None),
        P(DP, TP, None),
        P(DP, TP, None),
        P(DP),
        P(DP, None),
        P(DP),
        P(DP),
    )
    return jax.shard_map(
        shards,
        mesh=split,
        in_specs=placed,
        out_specs=(P(DP, TP, None), P(DP, None)),
        check_vma=False,
    )
```

```python
import functools

import jax
import jax.numpy as jnp
from jax import lax
from jax.experimental import pallas as pl
from jax.experimental.pallas import tpu as pltpu
from jax.sharding import Mesh
from jax.sharding import PartitionSpec as P

KVL = 512
PAGE = 64
CAP = 2
ARR = 16
RESMAX = 24
MAXROWS = 4
MOVES = 2
ROPE = 64
RES_POOL = 96
SHARES = 8
DP, TP = ("half", "group"), ("x", "core")
LATENT_ROWS = 5
META_LEFT, META_SLOT = 8, 16
ORDER = [y * 8 + z for y in range(7, -1, -1) for z in (7, 6, 5, 4, 0, 1, 2, 3)]
PEERS = list(range(7, -1, -1))
EPSILON = 1e-06
SCORE_SCALE = 192.0 ** (-0.5)
VMEM_LIMIT = 32 * 1024 * 1024

SMEM = functools.partial(pl.BlockSpec, memory_space=pltpu.SMEM)
VMEM = functools.partial(pl.BlockSpec, memory_space=pltpu.VMEM)
HBM = functools.partial(pl.BlockSpec, memory_space=pltpu.HBM)
ANY = functools.partial(pl.BlockSpec, memory_space=pl.ANY)


def normalize(raw_latent, kv_gain):
    head_part = raw_latent[:, :KVL]
    inverse = lax.rsqrt(jnp.mean(head_part * head_part, axis=1, keepdims=True) + EPSILON)
    return jnp.concatenate(
        [head_part * inverse * kv_gain[None, :], raw_latent[:, KVL:]], axis=1
    )


def served_order(give_ref):
    first, second = give_ref[0], give_ref[1]
    low, high = jnp.minimum(first, second), jnp.maximum(first, second)
    kept_low = jnp.where(low > 0, 0, jnp.where(high > 1, 1, 2))
    kept_high = jnp.where(high < 3, 3, jnp.where(low < 2, 2, 1))
    return [first, second, kept_low, kept_high]


def share_index():
    return lax.axis_index("x") * 2 + lax.axis_index("core")


def resident_count(length):
    return (length + (PAGE - 1)) // PAGE - ARR


def stacked(rows, start=0, count=8):
    place = lax.broadcasted_iota(jnp.int32, (count, 128), 0)
    result = jnp.zeros((count, 128), jnp.float32)
    for index, row in enumerate(rows):
        result = jnp.where(place == start + index, row, result)
    return result


def turned(rows):
    return jnp.concatenate([rows, jnp.zeros((128 - rows.shape[0], 128), jnp.float32)], axis=0).T


def coded(level):
    terms = []
    for _ in range(3):
        terms.append(level.astype(jnp.bfloat16).astype(jnp.float32))
        level = level - terms[-1]
    return terms


def decoded(stats, count):
    stats = stats.astype(jnp.float32)
    return stats[:count] + stats[count : 2 * count] + stats[2 * count : 3 * count]


def blended(weights, values):
    return lax.dot_general(weights, values, (((0,), (0,)), ((), ())), preferred_element_type=jnp.float32)


def pack_kernel(dest_hbm, outbox_ref, out_ref, page_ref, stage_ref, dest_ref, index_ref, in_sems, out_sems, dest_sem):
    sent, groups = outbox_ref.shape[0], out_ref.shape[0]
    parts = in_sems.shape[0]
    step = sent // parts
    dest_load = pltpu.make_async_copy(dest_hbm, dest_ref, dest_sem)
    dest_load.start()
    loads = [
        pltpu.make_async_copy(outbox_ref.at[pl.ds(i * step, step)], page_ref.at[pl.ds(i * step, step)], in_sems.at[i])
        for i in range(parts)
    ]
    for load in loads:
        load.start()
    page_ref[sent] = jnp.zeros_like(page_ref[sent])
    for i in range(groups * CAP):
        index_ref[i] = sent
    dest_load.wait()
    for i in range(sent):
        slot = dest_ref[i] * CAP
        index_ref[slot + (index_ref[slot] != sent).astype(jnp.int32)] = i
    for load in loads:
        load.wait()
    block = groups // out_sems.shape[0]
    stores = []
    for part in range(out_sems.shape[0]):
        for dest in range(part * block, (part + 1) * block):
            for rank in range(CAP):
                page = page_ref.at[index_ref[ORDER[dest] * CAP + rank]]
                stage_ref[dest, :, rank * KVL : (rank + 1) * KVL] = page[:, :KVL]
                stage_ref[dest, :, CAP * KVL + rank * ROPE : CAP * KVL + (rank + 1) * ROPE] = page[:, KVL:]
        span = pl.ds(part * block, block)
        store = pltpu.make_async_copy(stage_ref.at[span], out_ref.at[span], out_sems.at[part])
        store.start()
        stores.append(store)
    for store in stores:
        store.wait()


def resident_kernel(
    give_ref, table_ref, length_ref, places_ref, cache_ref, query_ref, latent_ref, meta_ref, stat_ref, handed_ref, place_ref, *refs
):
    query_outs, blend_out, key_ref = refs[:-2], refs[-2], refs[-1]
    piece = cache_ref.shape[1]
    shard = share_index()
    resident = RESMAX * piece
    order = served_order(give_ref)
    tops, totals, handed = [], [], []
    row_ids = lax.broadcasted_iota(jnp.int32, place_ref.shape, 0)
    places = jnp.zeros(place_ref.shape, jnp.int32)
    for place, row in enumerate(order):
        places = jnp.where(row_ids == row, place, places)
        query_outs[0][place] = query_ref[row]
        length = length_ref[row]
        count = resident_count(length)
        meta_ref[META_LEFT + place] = length - count * PAGE
        for entry in range(ARR):
            slot = table_ref[row, count + entry] - RES_POOL
            meta_ref[META_SLOT + place * ARR + entry] = places_ref[slot // CAP] * CAP + lax.rem(slot, CAP)
        for pair in range(RESMAX // 2):
            parts = []
            for half in range(2):
                entry = pair * 2 + half
                parts.append(cache_ref[table_ref[row, jnp.where(entry < count, entry, 0)]])
            key_ref[place, pair * 2 * piece : (pair + 1) * 2 * piece, :] = jnp.concatenate(parts, axis=0)
        latent = latent_ref[pl.ds(row, 1), :]
        key_ref[place, resident:, :] = jnp.broadcast_to(latent, (16, latent.shape[1])).astype(jnp.bfloat16)
        if place < MOVES:
            latent = jnp.concatenate([latent, jnp.zeros((1, 128 - ROPE), jnp.float32)], axis=1)
            handed.extend(latent[:, chunk * 128 : (chunk + 1) * 128] for chunk in range(LATENT_ROWS))
    handed_ref[...] = stacked(handed, 3 * MOVES, 16)
    place_ref[...] = places
    for place, row in enumerate(order):
        count = resident_count(length_ref[row])
        keys = key_ref[place]
        scores = SCORE_SCALE * jnp.dot(keys, query_outs[0][place], preferred_element_type=jnp.float32)
        token = lax.broadcasted_iota(jnp.int32, scores.shape, 0)
        fresh = jnp.where(shard == 0, resident, -1)
        scores = jnp.where((token < count * piece) | (token == fresh), scores, -jnp.inf)
        top = jnp.max(scores, axis=0, keepdims=True)
        weights = jnp.exp(scores - top)
        blend_out[place] = blended(weights.astype(jnp.bfloat16), keys[:, :KVL])
        tops.append(top)
        totals.append(jnp.sum(weights, axis=0, keepdims=True))
    stat_ref[...] = stacked(tops + totals)


def arrived_kernel(meta_hbm, blend_hbm, query_hbm, arrived_ref, stat_ref, *refs):
    mine_ref, other_ref, key_ref, rope_ref, blend_refs, query_refs, meta_ref, sems = refs
    loads = [pltpu.make_async_copy(meta_hbm, meta_ref, sems.at[MAXROWS])]
    query_loads = [pltpu.make_async_copy(query_hbm.at[place], query_refs.at[place], sems.at[MAXROWS + 1 + place]) for place in range(MAXROWS)]
    loads += [pltpu.make_async_copy(blend_hbm.at[place], blend_refs.at[place], sems.at[place]) for place in range(MAXROWS)]
    for load in loads[:1] + query_loads + loads[1:]:
        load.start()
    loads[0].wait()
    piece = arrived_ref.shape[1]
    rows, heads = MAXROWS, stat_ref.shape[1]
    own = heads // SHARES
    chips = SHARES // 2
    first_half = lax.broadcasted_iota(jnp.int32, (piece, 128), 1) // ROPE
    for place in range(rows):
        for pair in range(ARR // 2):
            latents, ropes = [], []
            for half in range(2):
                slot = meta_ref[META_SLOT + place * ARR + pair * 2 + half]
                source, rank = slot // CAP, lax.rem(slot, CAP)
                latents.append(arrived_ref[source, :, pl.ds(pl.multiple_of(rank * KVL, KVL), KVL)])
                both = arrived_ref[source, :, CAP * KVL : CAP * KVL + 128].astype(jnp.float32)
                ropes.append(jnp.where(first_half == rank, both, 0.0))
            span = slice(pair * 2 * piece, (pair + 1) * 2 * piece)
            key_ref[place, span, :] = jnp.concatenate(latents, axis=0)
            rope_ref[place, span, :] = jnp.concatenate(ropes, axis=0).astype(jnp.bfloat16)
    token = lax.broadcasted_iota(jnp.int32, (ARR * piece, heads), 0)
    position = token // piece * PAGE + share_index() * piece + lax.rem(token, piece)
    levels, shrinks, weights = [], [], []
    for load in query_loads:
        load.wait()
    for place in range(rows):
        query = query_refs[place]
        rope_query = jnp.concatenate([query[KVL:], query[KVL:]], axis=0)
        scores = jnp.dot(key_ref[place], query[:KVL], preferred_element_type=jnp.float32)
        scores += jnp.dot(rope_ref[place], rope_query, preferred_element_type=jnp.float32)
        scores = jnp.where(position < meta_ref[META_LEFT + place], SCORE_SCALE * scores, -jnp.inf)
        old_top, old_total = stat_ref[place : place + 1, :], stat_ref[MAXROWS + place : MAXROWS + place + 1, :]
        top = jnp.maximum(jnp.max(scores, axis=0, keepdims=True), old_top)
        shrink = jnp.exp(old_top - top)
        weight = jnp.exp(scores - top)
        total = jnp.sum(weight, axis=0, keepdims=True) + shrink * old_total
        inverse = 1.0 / total
        weights.append((weight * inverse).astype(jnp.bfloat16))
        shrinks.append(shrink * inverse)
        levels.append(top + jnp.log(total))
    columns = turned(stacked(shrinks))
    for load in loads[1:]:
        load.wait()
    even = lax.axis_index("core") == 0
    for place in range(rows):
        blend = blended(weights[place], key_ref[place])
        partial = (blend + columns[:, place : place + 1] * blend_refs[place]).astype(jnp.bfloat16)
        for chip in range(chips):
            block_even = partial[2 * chip * own : (2 * chip + 1) * own]
            block_odd = partial[(2 * chip + 1) * own : (2 * chip + 2) * own]
            block_mine = jnp.where(even, block_even, block_odd)
            block_other = jnp.where(even, block_odd, block_even)
            for chunk in range(KVL // 128):
                start = ((chip * (KVL // 128) + chunk) * rows + place) * own
                lanes = slice(chunk * 128, (chunk + 1) * 128)
                mine_ref[start : start + own, :] = block_mine[:, lanes]
                other_ref[start : start + own, :] = block_other[:, lanes]
    terms = coded(stacked(levels))
    stats = jnp.concatenate([terms[0][:rows], terms[1][:rows], terms[2][:rows], terms[0][rows:]], axis=0)
    stats = stats.astype(jnp.bfloat16)
    mine_ref[chips * (KVL // 128) * rows * own :, :] = stats
    other_ref[chips * (KVL // 128) * rows * own :, :] = stats


def merge_kernel(mine_ref, other_ref, handed_ref, send_ref, column_ref):
    chips = SHARES // 2
    rows, own = MAXROWS, (mine_ref.shape[0] - 16) // (chips * (KVL // 128) * MAXROWS)
    side = lax.axis_index("half")
    stat_base = chips * (KVL // 128) * rows * own
    level_a = decoded(mine_ref[stat_base:, :], rows)
    level_b = decoded(other_ref[stat_base:, :], rows)
    peak = jnp.maximum(level_a, level_b)
    weight_a, weight_b = jnp.exp(level_a - peak), jnp.exp(level_b - peak)
    total = weight_a + weight_b
    terms = coded(peak + jnp.log(total))
    inverse = 1.0 / total
    column_ref[...] = turned(jnp.concatenate([weight_a * inverse, weight_b * inverse], axis=0))
    core = lax.axis_index("core")
    stats = []
    for part in range(2):
        places = range(part * MOVES, (part + 1) * MOVES)
        kept = stacked([term[place : place + 1] for term in terms for place in places], 0, 16)
        stats.append((kept + handed_ref[...]).astype(jnp.bfloat16))
    for chip in range(chips):
        columns = column_ref[pl.ds(pl.multiple_of((2 * chip + core) * own, own), own), :]
        for part in range(2):
            target = jnp.where(side == part, PEERS.index(chips + chip), PEERS.index(chip))
            for move in range(MOVES):
                place = part * MOVES + move
                column_a = jnp.broadcast_to(columns[:, place : place + 1], (own, 128))
                column_b = jnp.broadcast_to(columns[:, rows + place : rows + place + 1], (own, 128))
                for chunk in range(KVL // 128):
                    start = ((chip * (KVL // 128) + chunk) * rows + place) * own
                    value = column_a * mine_ref[start : start + own, :].astype(jnp.float32)
                    value += column_b * other_ref[start : start + own, :].astype(jnp.float32)
                    to = (chunk * MOVES + move) * own
                    send_ref[target, to : to + own, :] = value.astype(jnp.bfloat16)
            send_ref[target, KVL // 128 * MOVES * own :, :] = stats[part]


def finish_kernel(received_ref, latent_ref, place_ref, out_ref, latent_out, column_ref):
    chips = SHARES // 2
    own = out_ref.shape[1]
    stat_base = KVL // 128 * MOVES * own
    side = lax.axis_index("half")
    sources, weights = [], []
    for part in range(2):
        sources.append(
            [jnp.where(side == part, PEERS.index(chips + chip), PEERS.index(chip)) for chip in range(chips)]
        )
        levels = [decoded(received_ref[source, stat_base:, :], MOVES) for source in sources[part]]
        peak = functools.reduce(jnp.maximum, levels)
        shares = [jnp.exp(level - peak) for level in levels]
        inverse = 1.0 / functools.reduce(lambda a, b: a + b, shares)
        weights.extend(share * inverse for share in shares)
    column_ref[...] = turned(jnp.concatenate(weights, axis=0))
    columns = column_ref[pl.ds(pl.multiple_of(share_index() * own, own), own), :]
    results = []
    for part in range(2):
        for move in range(MOVES):
            values = [0.0] * (KVL // 128)
            for chip in range(chips):
                lane = (part * chips + chip) * MOVES + move
                column = jnp.broadcast_to(columns[:, lane : lane + 1], (own, 128))
                for chunk in range(KVL // 128):
                    start = (chunk * MOVES + move) * own
                    block = received_ref[sources[part][chip], start : start + own, :].astype(jnp.float32)
                    values[chunk] = values[chunk] + column * block
            results.append(values)
    for row in range(MAXROWS):
        at = jnp.broadcast_to(place_ref[row : row + 1, :], (own, 128))
        for chunk in range(KVL // 128):
            value = results[MAXROWS - 1][chunk]
            for place in range(MAXROWS - 1):
                value = jnp.where(at == place, results[place][chunk], value)
            out_ref[row, :, chunk * 128 : (chunk + 1) * 128] = value.astype(jnp.bfloat16)
    taken = received_ref[sources[0][0], stat_base:, :].astype(jnp.float32)
    latent = latent_ref[...]
    rows, width = latent.shape
    at = jnp.concatenate([place_ref[:rows, :]] * LATENT_ROWS, axis=1)[:, :width]
    for move in range(MOVES):
        first = 3 * MOVES + move * LATENT_ROWS
        entry = jnp.concatenate([taken[first + chunk : first + chunk + 1] for chunk in range(LATENT_ROWS)], axis=1)
        latent = jnp.where(at == move, entry[:, :width], latent)
    latent_out[...] = latent.astype(jnp.bfloat16)


def shards(
    hidden,
    kva_weight,
    kv_gain,
    queries,
    latent_cache,
    outbox,
    out_dest,
    page_table,
    lengths,
    give_rows,
):
    group_count = lax.axis_size(DP)
    chip_count = lax.axis_size("x")
    row_count = hidden.shape[0]
    page_piece = latent_cache.shape[1]
    heads = queries.shape[1]
    own = heads // SHARES
    moves = give_rows.shape[0]
    query_t = jnp.swapaxes(queries, 1, 2)
    params = pltpu.CompilerParams(vmem_limit_bytes=VMEM_LIMIT)
    shape = jax.ShapeDtypeStruct
    in_hbm = functools.partial(pltpu.with_memory_space_constraint, memory_space=pltpu.HBM)

    outgoing = pl.pallas_call(
        pack_kernel,
        out_shape=shape((group_count, page_piece, CAP * (KVL + ROPE)), jnp.bfloat16),
        in_specs=[HBM(), HBM()],
        out_specs=ANY(),
        scratch_shapes=[
            pltpu.VMEM((outbox.shape[0] + 1,) + outbox.shape[1:], jnp.bfloat16),
            pltpu.VMEM((group_count, page_piece, CAP * (KVL + ROPE)), jnp.bfloat16),
            pltpu.SMEM(out_dest.shape, jnp.int32),
            pltpu.SMEM((group_count * CAP,), jnp.int32),
            pltpu.SemaphoreType.DMA((8,)),
            pltpu.SemaphoreType.DMA((8,)),
            pltpu.SemaphoreType.DMA,
        ],
        compiler_params=params,
        name="pack",
    )(in_hbm(out_dest), in_hbm(outbox))
    arrived = lax.all_to_all(outgoing, DP, split_axis=0, concat_axis=0, tiled=True, axis_index_groups=[ORDER])

    partial_raw = jnp.dot(hidden, kva_weight, preferred_element_type=jnp.float32)
    parts = lax.all_gather(partial_raw, TP)
    latent = lax.reduce_precision(normalize(jnp.sum(parts, axis=0), kv_gain), 8, 7)

    places = [0] * group_count
    for place, group in enumerate(ORDER):
        places[group] = place
    meta, stats, handed, place, *operands, blend = pl.pallas_call(
        resident_kernel,
        out_shape=(
            shape((128,), jnp.int32),
            shape((2 * MAXROWS, heads), jnp.float32),
            shape((16, 128), jnp.float32),
            shape((8, 128), jnp.int32),
        )
        + (shape(query_t.shape, jnp.bfloat16),)
        + (shape((row_count, heads, KVL), jnp.float32),),
        in_specs=[SMEM()] * 4 + [VMEM()] * 3,
        out_specs=(SMEM(),) + (VMEM(),) * 5,
        scratch_shapes=[pltpu.VMEM((row_count, RESMAX * page_piece + 16, latent_cache.shape[2]), jnp.bfloat16)],
        compiler_params=params,
        name="resident",
    )(give_rows, page_table, lengths, jnp.array(places, jnp.int32), latent_cache, query_t, latent)

    part_shape = shape((chip_count * (KVL // 128) * row_count * own + 16, 128), jnp.bfloat16)
    mine, other = pl.pallas_call(
        arrived_kernel,
        out_shape=(part_shape, part_shape),
        in_specs=[HBM()] * 3 + [VMEM()] * 2,
        out_specs=(VMEM(), VMEM()),
        scratch_shapes=[
            pltpu.VMEM((row_count, ARR * page_piece, KVL), jnp.bfloat16),
            pltpu.VMEM((row_count, ARR * page_piece, 128), jnp.bfloat16),
            pltpu.VMEM((row_count, heads, KVL), jnp.float32),
            pltpu.VMEM(query_t.shape, jnp.bfloat16),
            pltpu.SMEM((128,), jnp.int32),
            pltpu.SemaphoreType.DMA((2 * row_count + 1,)),
        ],
        compiler_params=params,
        name="arrived",
    )(in_hbm(meta), in_hbm(blend), in_hbm(operands[0]), arrived, stats)
    other = lax.ppermute(other, "core", [(0, 1), (1, 0)])
    outbound = pl.pallas_call(
        merge_kernel,
        out_shape=shape((2 * chip_count, KVL // 128 * moves * own + 16, 128), jnp.bfloat16),
        in_specs=[VMEM()] * 3,
        out_specs=VMEM(),
        scratch_shapes=[pltpu.VMEM((heads, 128), jnp.float32)],
        compiler_params=params,
        name="merge",
    )(mine, other, handed)
    received = lax.all_to_all(
        outbound, ("half", "x"), split_axis=0, concat_axis=0, tiled=True, axis_index_groups=[PEERS]
    )
    return pl.pallas_call(
        finish_kernel,
        out_shape=(
            shape((row_count, own, KVL), jnp.bfloat16),
            shape(latent.shape, jnp.bfloat16),
        ),
        in_specs=[VMEM()] * 3,
        out_specs=(VMEM(), VMEM()),
        scratch_shapes=[pltpu.VMEM((heads, 128), jnp.float32)],
        compiler_params=params,
        name="finish",
    )(received, latent, place)


def solution(mesh):
    groups, shares = mesh.devices.shape
    split = Mesh(mesh.devices.reshape(2, groups // 2, shares // 2, 2), DP + TP)
    placed = (
        P(DP, TP),
        P(TP, None),
        P(),
        P(DP, None, None),
        P(DP, TP, None),
        P(DP, TP, None),
        P(DP),
        P(DP, None),
        P(DP),
        P(DP),
    )
    return jax.shard_map(
        shards,
        mesh=split,
        in_specs=placed,
        out_specs=(P(DP, TP, None), P(DP, None)),
        check_vma=False,
    )
```

```python
import functools

import jax
import jax.numpy as jnp
from jax import lax
from jax.experimental import pallas as pl
from jax.experimental.pallas import tpu as pltpu
from jax.sharding import Mesh
from jax.sharding import PartitionSpec as P

KVL = 512
PAGE = 64
CAP = 2
ARR = 16
RESMAX = 24
MAXROWS = 4
MOVES = 2
ROPE = 64
RES_POOL = 96
SHARES = 8
DP, TP = ("half", "group"), ("x", "core")
LATENT_ROWS = 5
META_LEFT, META_SLOT = 8, 16
ORDER = [y * 8 + z for y in range(7, -1, -1) for z in (7, 6, 5, 0, 1, 2, 3, 4)]
PEERS = list(range(7, -1, -1))
EPSILON = 1e-06
SCORE_SCALE = 192.0 ** (-0.5)
VMEM_LIMIT = 32 * 1024 * 1024

SMEM = functools.partial(pl.BlockSpec, memory_space=pltpu.SMEM)
VMEM = functools.partial(pl.BlockSpec, memory_space=pltpu.VMEM)
HBM = functools.partial(pl.BlockSpec, memory_space=pltpu.HBM)
ANY = functools.partial(pl.BlockSpec, memory_space=pl.ANY)


def normalize(raw_latent, kv_gain):
    head_part = raw_latent[:, :KVL]
    inverse = lax.rsqrt(jnp.mean(head_part * head_part, axis=1, keepdims=True) + EPSILON)
    return jnp.concatenate(
        [head_part * inverse * kv_gain[None, :], raw_latent[:, KVL:]], axis=1
    )


def served_order(give_ref):
    first, second = give_ref[0], give_ref[1]
    low, high = jnp.minimum(first, second), jnp.maximum(first, second)
    kept_low = jnp.where(low > 0, 0, jnp.where(high > 1, 1, 2))
    kept_high = jnp.where(high < 3, 3, jnp.where(low < 2, 2, 1))
    return [first, second, kept_low, kept_high]


def share_index():
    return lax.axis_index("x") * 2 + lax.axis_index("core")


def resident_count(length):
    return (length + (PAGE - 1)) // PAGE - ARR


def stacked(rows, start=0, count=8):
    place = lax.broadcasted_iota(jnp.int32, (count, 128), 0)
    result = jnp.zeros((count, 128), jnp.float32)
    for index, row in enumerate(rows):
        result = jnp.where(place == start + index, row, result)
    return result


def turned(rows):
    return jnp.concatenate([rows, jnp.zeros((128 - rows.shape[0], 128), jnp.float32)], axis=0).T


def coded(level):
    terms = []
    for _ in range(3):
        terms.append(level.astype(jnp.bfloat16).astype(jnp.float32))
        level = level - terms[-1]
    return terms


def decoded(stats, count):
    stats = stats.astype(jnp.float32)
    return stats[:count] + stats[count : 2 * count] + stats[2 * count : 3 * count]


def blended(weights, values):
    return lax.dot_general(weights, values, (((0,), (0,)), ((), ())), preferred_element_type=jnp.float32)


def pack_kernel(dest_hbm, outbox_ref, out_ref, page_ref, stage_ref, dest_ref, index_ref, in_sems, out_sems, dest_sem):
    sent, groups = outbox_ref.shape[0], out_ref.shape[0]
    parts = in_sems.shape[0]
    step = sent // parts
    dest_load = pltpu.make_async_copy(dest_hbm, dest_ref, dest_sem)
    dest_load.start()
    loads = [
        pltpu.make_async_copy(outbox_ref.at[pl.ds(i * step, step)], page_ref.at[pl.ds(i * step, step)], in_sems.at[i])
        for i in range(parts)
    ]
    for load in loads:
        load.start()
    page_ref[sent] = jnp.zeros_like(page_ref[sent])
    for i in range(groups * CAP):
        index_ref[i] = sent
    dest_load.wait()
    for i in range(sent):
        slot = dest_ref[i] * CAP
        index_ref[slot + (index_ref[slot] != sent).astype(jnp.int32)] = i
    for load in loads:
        load.wait()
    block = groups // out_sems.shape[0]
    stores = []
    for part in range(out_sems.shape[0]):
        for dest in range(part * block, (part + 1) * block):
            ropes = []
            for rank in range(CAP):
                page = page_ref.at[index_ref[ORDER[dest] * CAP + rank]]
                stage_ref[dest, :, rank * KVL : (rank + 1) * KVL] = page[:, :KVL]
                ropes.append(page[:, KVL:])
            stage_ref[dest, :, CAP * KVL :] = jnp.concatenate(ropes, axis=1)
        span = pl.ds(part * block, block)
        store = pltpu.make_async_copy(stage_ref.at[span], out_ref.at[span], out_sems.at[part])
        store.start()
        stores.append(store)
    for store in stores:
        store.wait()


def resident_kernel(
    give_ref, table_ref, length_ref, places_ref, cache_ref, query_ref, latent_ref, meta_ref, stat_ref, handed_ref, place_ref, *refs
):
    query_outs, blend_out, key_ref = refs[:-2], refs[-2], refs[-1]
    piece = cache_ref.shape[1]
    shard = share_index()
    resident = RESMAX * piece
    order = served_order(give_ref)
    tops, totals, handed = [], [], []
    row_ids = lax.broadcasted_iota(jnp.int32, place_ref.shape, 0)
    places = jnp.zeros(place_ref.shape, jnp.int32)
    for place, row in enumerate(order):
        places = jnp.where(row_ids == row, place, places)
        query_outs[0][place] = query_ref[row]
        length = length_ref[row]
        count = resident_count(length)
        meta_ref[META_LEFT + place] = length - count * PAGE
        for entry in range(ARR):
            slot = table_ref[row, count + entry] - RES_POOL
            meta_ref[META_SLOT + place * ARR + entry] = places_ref[slot // CAP] * CAP + lax.rem(slot, CAP)
        for pair in range(RESMAX // 2):
            parts = []
            for half in range(2):
                entry = pair * 2 + half
                parts.append(cache_ref[table_ref[row, jnp.where(entry < count, entry, 0)]])
            key_ref[place, pair * 2 * piece : (pair + 1) * 2 * piece, :] = jnp.concatenate(parts, axis=0)
        latent = latent_ref[pl.ds(row, 1), :]
        key_ref[place, resident:, :] = jnp.broadcast_to(latent, (16, latent.shape[1])).astype(jnp.bfloat16)
        if place < MOVES:
            latent = jnp.concatenate([latent, jnp.zeros((1, 128 - ROPE), jnp.float32)], axis=1)
            handed.extend(latent[:, chunk * 128 : (chunk + 1) * 128] for chunk in range(LATENT_ROWS))
    handed_ref[...] = stacked(handed, 3 * MOVES, 16)
    place_ref[...] = places
    for place, row in enumerate(order):
        count = resident_count(length_ref[row])
        keys = key_ref[place]
        scores = SCORE_SCALE * jnp.dot(keys, query_outs[0][place], preferred_element_type=jnp.float32)
        token = lax.broadcasted_iota(jnp.int32, scores.shape, 0)
        fresh = jnp.where(shard == 0, resident, -1)
        scores = jnp.where((token < count * piece) | (token == fresh), scores, -jnp.inf)
        top = jnp.max(scores, axis=0, keepdims=True)
        weights = jnp.exp(scores - top)
        blend_out[place] = blended(weights.astype(jnp.bfloat16), keys[:, :KVL])
        tops.append(top)
        totals.append(jnp.sum(weights, axis=0, keepdims=True))
    stat_ref[...] = stacked(tops + totals)


def arrived_kernel(meta_hbm, blend_hbm, query_hbm, arrived_ref, stat_ref, *refs):
    mine_ref, other_ref, key_ref, rope_ref, blend_refs, query_refs, meta_ref, sems = refs
    loads = [pltpu.make_async_copy(meta_hbm, meta_ref, sems.at[MAXROWS])]
    query_loads = [pltpu.make_async_copy(query_hbm.at[place], query_refs.at[place], sems.at[MAXROWS + 1 + place]) for place in range(MAXROWS)]
    loads += [pltpu.make_async_copy(blend_hbm.at[place], blend_refs.at[place], sems.at[place]) for place in range(MAXROWS)]
    for load in loads[:1] + query_loads + loads[1:]:
        load.start()
    loads[0].wait()
    piece = arrived_ref.shape[1]
    rows, heads = MAXROWS, stat_ref.shape[1]
    own = heads // SHARES
    chips = SHARES // 2
    first_half = lax.broadcasted_iota(jnp.int32, (piece, 128), 1) // ROPE
    for place in range(rows):
        for pair in range(ARR // 2):
            latents, ropes = [], []
            for half in range(2):
                slot = meta_ref[META_SLOT + place * ARR + pair * 2 + half]
                source, rank = slot // CAP, lax.rem(slot, CAP)
                latents.append(arrived_ref[source, :, pl.ds(pl.multiple_of(rank * KVL, KVL), KVL)])
                both = arrived_ref[source, :, CAP * KVL : CAP * KVL + 128].astype(jnp.float32)
                ropes.append(jnp.where(first_half == rank, both, 0.0))
            span = slice(pair * 2 * piece, (pair + 1) * 2 * piece)
            key_ref[place, span, :] = jnp.concatenate(latents, axis=0)
            rope_ref[place, span, :] = jnp.concatenate(ropes, axis=0).astype(jnp.bfloat16)
    token = lax.broadcasted_iota(jnp.int32, (ARR * piece, heads), 0)
    position = token // piece * PAGE + share_index() * piece + lax.rem(token, piece)
    levels, shrinks, weights = [], [], []
    for load in query_loads:
        load.wait()
    for place in range(rows):
        query = query_refs[place]
        rope_query = jnp.concatenate([query[KVL:], query[KVL:]], axis=0)
        scores = jnp.dot(key_ref[place], query[:KVL], preferred_element_type=jnp.float32)
        scores += jnp.dot(rope_ref[place], rope_query, preferred_element_type=jnp.float32)
        scores = jnp.where(position < meta_ref[META_LEFT + place], SCORE_SCALE * scores, -jnp.inf)
        old_top, old_total = stat_ref[place : place + 1, :], stat_ref[MAXROWS + place : MAXROWS + place + 1, :]
        top = jnp.maximum(jnp.max(scores, axis=0, keepdims=True), old_top)
        shrink = jnp.exp(old_top - top)
        weight = jnp.exp(scores - top)
        total = jnp.sum(weight, axis=0, keepdims=True) + shrink * old_total
        inverse = 1.0 / total
        weights.append((weight * inverse).astype(jnp.bfloat16))
        shrinks.append(shrink * inverse)
        levels.append(top + jnp.log(total))
    columns = turned(stacked(shrinks))
    for load in loads[1:]:
        load.wait()
    even = lax.axis_index("core") == 0
    for place in range(rows):
        blend = blended(weights[place], key_ref[place])
        partial = (blend + columns[:, place : place + 1] * blend_refs[place]).astype(jnp.bfloat16)
        for chip in range(chips):
            block_even = partial[2 * chip * own : (2 * chip + 1) * own]
            block_odd = partial[(2 * chip + 1) * own : (2 * chip + 2) * own]
            block_mine = jnp.where(even, block_even, block_odd)
            block_other = jnp.where(even, block_odd, block_even)
            for chunk in range(KVL // 128):
                start = ((chip * (KVL // 128) + chunk) * rows + place) * own
                lanes = slice(chunk * 128, (chunk + 1) * 128)
                mine_ref[start : start + own, :] = block_mine[:, lanes]
                other_ref[start : start + own, :] = block_other[:, lanes]
    terms = coded(stacked(levels))
    stats = jnp.concatenate([terms[0][:rows], terms[1][:rows], terms[2][:rows], terms[0][rows:]], axis=0)
    stats = stats.astype(jnp.bfloat16)
    mine_ref[chips * (KVL // 128) * rows * own :, :] = stats
    other_ref[chips * (KVL // 128) * rows * own :, :] = stats


def merge_kernel(mine_ref, other_ref, handed_ref, send_ref, column_ref):
    chips = SHARES // 2
    rows, own = MAXROWS, (mine_ref.shape[0] - 16) // (chips * (KVL // 128) * MAXROWS)
    side = lax.axis_index("half")
    stat_base = chips * (KVL // 128) * rows * own
    level_a = decoded(mine_ref[stat_base:, :], rows)
    level_b = decoded(other_ref[stat_base:, :], rows)
    peak = jnp.maximum(level_a, level_b)
    weight_a, weight_b = jnp.exp(level_a - peak), jnp.exp(level_b - peak)
    total = weight_a + weight_b
    terms = coded(peak + jnp.log(total))
    inverse = 1.0 / total
    column_ref[...] = turned(jnp.concatenate([weight_a * inverse, weight_b * inverse], axis=0))
    core = lax.axis_index("core")
    stats = []
    for part in range(2):
        places = range(part * MOVES, (part + 1) * MOVES)
        kept = stacked([term[place : place + 1] for term in terms for place in places], 0, 16)
        stats.append((kept + handed_ref[...]).astype(jnp.bfloat16))
    for chip in range(chips):
        columns = column_ref[pl.ds(pl.multiple_of((2 * chip + core) * own, own), own), :]
        for part in range(2):
            target = jnp.where(side == part, PEERS.index(chips + chip), PEERS.index(chip))
            for move in range(MOVES):
                place = part * MOVES + move
                column_a = jnp.broadcast_to(columns[:, place : place + 1], (own, 128))
                column_b = jnp.broadcast_to(columns[:, rows + place : rows + place + 1], (own, 128))
                for chunk in range(KVL // 128):
                    start = ((chip * (KVL // 128) + chunk) * rows + place) * own
                    value = column_a * mine_ref[start : start + own, :].astype(jnp.float32)
                    value += column_b * other_ref[start : start + own, :].astype(jnp.float32)
                    to = (chunk * MOVES + move) * own
                    send_ref[target, to : to + own, :] = value.astype(jnp.bfloat16)
            send_ref[target, KVL // 128 * MOVES * own :, :] = stats[part]


def finish_kernel(received_ref, latent_ref, place_ref, out_ref, latent_out, column_ref):
    chips = SHARES // 2
    own = out_ref.shape[1]
    stat_base = KVL // 128 * MOVES * own
    side = lax.axis_index("half")
    sources, weights = [], []
    for part in range(2):
        sources.append(
            [jnp.where(side == part, PEERS.index(chips + chip), PEERS.index(chip)) for chip in range(chips)]
        )
        levels = [decoded(received_ref[source, stat_base:, :], MOVES) for source in sources[part]]
        peak = functools.reduce(jnp.maximum, levels)
        shares = [jnp.exp(level - peak) for level in levels]
        inverse = 1.0 / functools.reduce(lambda a, b: a + b, shares)
        weights.extend(share * inverse for share in shares)
    column_ref[...] = turned(jnp.concatenate(weights, axis=0))
    columns = column_ref[pl.ds(pl.multiple_of(share_index() * own, own), own), :]
    results = []
    for part in range(2):
        for move in range(MOVES):
            values = [0.0] * (KVL // 128)
            for chip in range(chips):
                lane = (part * chips + chip) * MOVES + move
                column = jnp.broadcast_to(columns[:, lane : lane + 1], (own, 128))
                for chunk in range(KVL // 128):
                    start = (chunk * MOVES + move) * own
                    block = received_ref[sources[part][chip], start : start + own, :].astype(jnp.float32)
                    values[chunk] = values[chunk] + column * block
            results.append(values)
    for row in range(MAXROWS):
        at = jnp.broadcast_to(place_ref[row : row + 1, :], (own, 128))
        for chunk in range(KVL // 128):
            value = results[MAXROWS - 1][chunk]
            for place in range(MAXROWS - 1):
                value = jnp.where(at == place, results[place][chunk], value)
            out_ref[row, :, chunk * 128 : (chunk + 1) * 128] = value.astype(jnp.bfloat16)
    taken = received_ref[sources[0][0], stat_base:, :].astype(jnp.float32)
    latent = latent_ref[...]
    rows, width = latent.shape
    at = jnp.concatenate([place_ref[:rows, :]] * LATENT_ROWS, axis=1)[:, :width]
    for move in range(MOVES):
        first = 3 * MOVES + move * LATENT_ROWS
        entry = jnp.concatenate([taken[first + chunk : first + chunk + 1] for chunk in range(LATENT_ROWS)], axis=1)
        latent = jnp.where(at == move, entry[:, :width], latent)
    latent_out[...] = latent.astype(jnp.bfloat16)


def shards(
    hidden,
    kva_weight,
    kv_gain,
    queries,
    latent_cache,
    outbox,
    out_dest,
    page_table,
    lengths,
    give_rows,
):
    group_count = lax.axis_size(DP)
    chip_count = lax.axis_size("x")
    row_count = hidden.shape[0]
    page_piece = latent_cache.shape[1]
    heads = queries.shape[1]
    own = heads // SHARES
    moves = give_rows.shape[0]
    query_t = jnp.swapaxes(queries, 1, 2)
    params = pltpu.CompilerParams(vmem_limit_bytes=VMEM_LIMIT)
    shape = jax.ShapeDtypeStruct
    in_hbm = functools.partial(pltpu.with_memory_space_constraint, memory_space=pltpu.HBM)

    outgoing = pl.pallas_call(
        pack_kernel,
        out_shape=shape((group_count, page_piece, CAP * (KVL + ROPE)), jnp.bfloat16),
        in_specs=[HBM(), HBM()],
        out_specs=ANY(),
        scratch_shapes=[
            pltpu.VMEM((outbox.shape[0] + 1,) + outbox.shape[1:], jnp.bfloat16),
            pltpu.VMEM((group_count, page_piece, CAP * (KVL + ROPE)), jnp.bfloat16),
            pltpu.SMEM(out_dest.shape, jnp.int32),
            pltpu.SMEM((group_count * CAP,), jnp.int32),
            pltpu.SemaphoreType.DMA((2,)),
            pltpu.SemaphoreType.DMA((4,)),
            pltpu.SemaphoreType.DMA,
        ],
        compiler_params=params,
        name="pack",
    )(in_hbm(out_dest), in_hbm(outbox))
    arrived = lax.all_to_all(outgoing, DP, split_axis=0, concat_axis=0, tiled=True, axis_index_groups=[ORDER])

    partial_raw = jnp.dot(hidden, kva_weight, preferred_element_type=jnp.float32)
    parts = lax.all_gather(partial_raw, TP)
    latent = lax.reduce_precision(normalize(jnp.sum(parts, axis=0), kv_gain), 8, 7)

    places = [0] * group_count
    for place, group in enumerate(ORDER):
        places[group] = place
    meta, stats, handed, place, *operands, blend = pl.pallas_call(
        resident_kernel,
        out_shape=(
            shape((128,), jnp.int32),
            shape((2 * MAXROWS, heads), jnp.float32),
            shape((16, 128), jnp.float32),
            shape((8, 128), jnp.int32),
        )
        + (shape(query_t.shape, jnp.bfloat16),)
        + (shape((row_count, heads, KVL), jnp.float32),),
        in_specs=[SMEM()] * 4 + [VMEM()] * 3,
        out_specs=(SMEM(),) + (VMEM(),) * 5,
        scratch_shapes=[pltpu.VMEM((row_count, RESMAX * page_piece + 16, latent_cache.shape[2]), jnp.bfloat16)],
        compiler_params=params,
        name="resident",
    )(give_rows, page_table, lengths, jnp.array(places, jnp.int32), latent_cache, query_t, latent)

    part_shape = shape((chip_count * (KVL // 128) * row_count * own + 16, 128), jnp.bfloat16)
    mine, other = pl.pallas_call(
        arrived_kernel,
        out_shape=(part_shape, part_shape),
        in_specs=[HBM()] * 3 + [VMEM()] * 2,
        out_specs=(VMEM(), VMEM()),
        scratch_shapes=[
            pltpu.VMEM((row_count, ARR * page_piece, KVL), jnp.bfloat16),
            pltpu.VMEM((row_count, ARR * page_piece, 128), jnp.bfloat16),
            pltpu.VMEM((row_count, heads, KVL), jnp.float32),
            pltpu.VMEM(query_t.shape, jnp.bfloat16),
            pltpu.SMEM((128,), jnp.int32),
            pltpu.SemaphoreType.DMA((2 * row_count + 1,)),
        ],
        compiler_params=params,
        name="arrived",
    )(in_hbm(meta), in_hbm(blend), in_hbm(operands[0]), arrived, stats)
    other = lax.ppermute(other, "core", [(0, 1), (1, 0)])
    outbound = pl.pallas_call(
        merge_kernel,
        out_shape=shape((2 * chip_count, KVL // 128 * moves * own + 16, 128), jnp.bfloat16),
        in_specs=[VMEM()] * 3,
        out_specs=VMEM(),
        scratch_shapes=[pltpu.VMEM((heads, 128), jnp.float32)],
        compiler_params=params,
        name="merge",
    )(mine, other, handed)
    received = lax.all_to_all(
        outbound, ("half", "x"), split_axis=0, concat_axis=0, tiled=True, axis_index_groups=[PEERS]
    )
    return pl.pallas_call(
        finish_kernel,
        out_shape=(
            shape((row_count, own, KVL), jnp.bfloat16),
            shape(latent.shape, jnp.bfloat16),
        ),
        in_specs=[VMEM()] * 3,
        out_specs=(VMEM(), VMEM()),
        scratch_shapes=[pltpu.VMEM((heads, 128), jnp.float32)],
        compiler_params=params,
        name="finish",
    )(received, latent, place)


def solution(mesh):
    groups, shares = mesh.devices.shape
    split = Mesh(mesh.devices.reshape(2, groups // 2, shares // 2, 2), DP + TP)
    placed = (
        P(DP, TP),
        P(TP, None),
        P(),
        P(DP, None, None),
        P(DP, TP, None),
        P(DP, TP, None),
        P(DP),
        P(DP, None),
        P(DP),
        P(DP),
    )
    return jax.shard_map(
        shards,
        mesh=split,
        in_specs=placed,
        out_specs=(P(DP, TP, None), P(DP, None)),
        check_vma=False,
    )
```

```python
import functools

import jax
import jax.numpy as jnp
from jax import lax
from jax.experimental import pallas as pl
from jax.experimental.pallas import tpu as pltpu
from jax.sharding import Mesh
from jax.sharding import PartitionSpec as P

KVL = 512
PAGE = 64
CAP = 2
ARR = 16
RESMAX = 24
MAXROWS = 4
MOVES = 2
ROPE = 64
RES_POOL = 96
SHARES = 8
DP, TP = ("half", "group"), ("x", "core")
LATENT_ROWS = 5
META_LEFT, META_SLOT = 8, 16
ORDER = [y * 8 + z for y in range(7, -1, -1) for z in (7, 6, 5, 0, 1, 2, 3, 4)]
PEERS = list(range(7, -1, -1))
EPSILON = 1e-06
SCORE_SCALE = 192.0 ** (-0.5)
VMEM_LIMIT = 32 * 1024 * 1024

SMEM = functools.partial(pl.BlockSpec, memory_space=pltpu.SMEM)
VMEM = functools.partial(pl.BlockSpec, memory_space=pltpu.VMEM)
HBM = functools.partial(pl.BlockSpec, memory_space=pltpu.HBM)
ANY = functools.partial(pl.BlockSpec, memory_space=pl.ANY)


def normalize(raw_latent, kv_gain):
    head_part = raw_latent[:, :KVL]
    inverse = lax.rsqrt(jnp.mean(head_part * head_part, axis=1, keepdims=True) + EPSILON)
    return jnp.concatenate(
        [head_part * inverse * kv_gain[None, :], raw_latent[:, KVL:]], axis=1
    )


def served_order(give_ref):
    first, second = give_ref[0], give_ref[1]
    low, high = jnp.minimum(first, second), jnp.maximum(first, second)
    kept_low = jnp.where(low > 0, 0, jnp.where(high > 1, 1, 2))
    kept_high = jnp.where(high < 3, 3, jnp.where(low < 2, 2, 1))
    return [first, second, kept_low, kept_high]


def share_index():
    return lax.axis_index("x") * 2 + lax.axis_index("core")


def resident_count(length):
    return (length + (PAGE - 1)) // PAGE - ARR


def stacked(rows, start=0, count=8):
    place = lax.broadcasted_iota(jnp.int32, (count, 128), 0)
    result = jnp.zeros((count, 128), jnp.float32)
    for index, row in enumerate(rows):
        result = jnp.where(place == start + index, row, result)
    return result


def turned(rows):
    return jnp.concatenate([rows, jnp.zeros((128 - rows.shape[0], 128), jnp.float32)], axis=0).T


def coded(level):
    terms = []
    for _ in range(3):
        terms.append(level.astype(jnp.bfloat16).astype(jnp.float32))
        level = level - terms[-1]
    return terms


def decoded(stats, count):
    stats = stats.astype(jnp.float32)
    return stats[:count] + stats[count : 2 * count] + stats[2 * count : 3 * count]


def blended(weights, values):
    return lax.dot_general(weights, values, (((0,), (0,)), ((), ())), preferred_element_type=jnp.float32)


def pack_kernel(dest_hbm, outbox_ref, out_ref, page_ref, stage_ref, dest_ref, index_ref, in_sems, out_sems, dest_sem):
    sent, groups = outbox_ref.shape[0], out_ref.shape[0]
    parts = in_sems.shape[0]
    step = sent // parts
    dest_load = pltpu.make_async_copy(dest_hbm, dest_ref, dest_sem)
    dest_load.start()
    loads = [
        pltpu.make_async_copy(outbox_ref.at[pl.ds(i * step, step)], page_ref.at[pl.ds(i * step, step)], in_sems.at[i])
        for i in range(parts)
    ]
    for load in loads:
        load.start()
    page_ref[sent] = jnp.zeros_like(page_ref[sent])
    for i in range(groups * CAP):
        index_ref[i] = sent
    dest_load.wait()
    for i in range(sent):
        slot = dest_ref[i] * CAP
        index_ref[slot + (index_ref[slot] != sent).astype(jnp.int32)] = i
    for load in loads:
        load.wait()
    block = groups // out_sems.shape[0]
    stores = []
    for part in range(out_sems.shape[0]):
        for dest in range(part * block, (part + 1) * block):
            ropes = []
            for rank in range(CAP):
                page = page_ref.at[index_ref[ORDER[dest] * CAP + rank]]
                stage_ref[dest, :, rank * KVL : (rank + 1) * KVL] = page[:, :KVL]
                ropes.append(page[:, KVL:])
            stage_ref[dest, :, CAP * KVL :] = jnp.concatenate(ropes, axis=1)
        span = pl.ds(part * block, block)
        store = pltpu.make_async_copy(stage_ref.at[span], out_ref.at[span], out_sems.at[part])
        store.start()
        stores.append(store)
    for store in stores:
        store.wait()


def resident_kernel(
    give_ref, table_ref, length_ref, places_ref, cache_ref, query_ref, latent_ref, meta_ref, stat_ref, handed_ref, place_ref, *refs
):
    query_outs, blend_out, key_ref = refs[:-2], refs[-2], refs[-1]
    piece = cache_ref.shape[1]
    shard = share_index()
    resident = RESMAX * piece
    order = served_order(give_ref)
    tops, totals, handed = [], [], []
    row_ids = lax.broadcasted_iota(jnp.int32, place_ref.shape, 0)
    places = jnp.zeros(place_ref.shape, jnp.int32)
    for place, row in enumerate(order):
        places = jnp.where(row_ids == row, place, places)
        query_outs[0][place] = query_ref[row]
        length = length_ref[row]
        count = resident_count(length)
        meta_ref[META_LEFT + place] = length - count * PAGE
        for entry in range(ARR):
            slot = table_ref[row, count + entry] - RES_POOL
            meta_ref[META_SLOT + place * ARR + entry] = places_ref[slot // CAP] * CAP + lax.rem(slot, CAP)
        for pair in range(RESMAX // 2):
            parts = []
            for half in range(2):
                entry = pair * 2 + half
                parts.append(cache_ref[table_ref[row, jnp.where(entry < count, entry, 0)]])
            key_ref[place, pair * 2 * piece : (pair + 1) * 2 * piece, :] = jnp.concatenate(parts, axis=0)
        latent = latent_ref[pl.ds(row, 1), :]
        key_ref[place, resident:, :] = jnp.broadcast_to(latent, (16, latent.shape[1])).astype(jnp.bfloat16)
        if place < MOVES:
            latent = jnp.concatenate([latent, jnp.zeros((1, 128 - ROPE), jnp.float32)], axis=1)
            handed.extend(latent[:, chunk * 128 : (chunk + 1) * 128] for chunk in range(LATENT_ROWS))
    handed_ref[...] = stacked(handed, 3 * MOVES, 16)
    place_ref[...] = places
    for place, row in enumerate(order):
        count = resident_count(length_ref[row])
        keys = key_ref[place]
        scores = SCORE_SCALE * jnp.dot(keys, query_outs[0][place], preferred_element_type=jnp.float32)
        token = lax.broadcasted_iota(jnp.int32, scores.shape, 0)
        fresh = jnp.where(shard == 0, resident, -1)
        scores = jnp.where((token < count * piece) | (token == fresh), scores, -jnp.inf)
        top = jnp.max(scores, axis=0, keepdims=True)
        weights = jnp.exp(scores - top)
        blend_out[place] = blended(weights.astype(jnp.bfloat16), keys[:, :KVL])
        tops.append(top)
        totals.append(jnp.sum(weights, axis=0, keepdims=True))
    stat_ref[...] = stacked(tops + totals)


def arrived_kernel(meta_hbm, blend_hbm, query_hbm, arrived_ref, stat_ref, *refs):
    mine_ref, other_ref, key_ref, rope_ref, blend_refs, query_refs, meta_ref, sems = refs
    loads = [pltpu.make_async_copy(meta_hbm, meta_ref, sems.at[MAXROWS])]
    query_loads = [pltpu.make_async_copy(query_hbm.at[place], query_refs.at[place], sems.at[MAXROWS + 1 + place]) for place in range(MAXROWS)]
    loads += [pltpu.make_async_copy(blend_hbm.at[place], blend_refs.at[place], sems.at[place]) for place in range(MAXROWS)]
    for load in loads[:1] + query_loads + loads[1:]:
        load.start()
    loads[0].wait()
    piece = arrived_ref.shape[1]
    rows, heads = MAXROWS, stat_ref.shape[1]
    own = heads // SHARES
    chips = SHARES // 2
    first_half = lax.broadcasted_iota(jnp.int32, (piece, 128), 1) // ROPE
    for place in range(rows):
        for pair in range(ARR // 2):
            latents, ropes = [], []
            for half in range(2):
                slot = meta_ref[META_SLOT + place * ARR + pair * 2 + half]
                source, rank = slot // CAP, lax.rem(slot, CAP)
                latents.append(arrived_ref[source, :, pl.ds(pl.multiple_of(rank * KVL, KVL), KVL)])
                both = arrived_ref[source, :, CAP * KVL : CAP * KVL + 128].astype(jnp.float32)
                ropes.append(jnp.where(first_half == rank, both, 0.0))
            span = slice(pair * 2 * piece, (pair + 1) * 2 * piece)
            key_ref[place, span, :] = jnp.concatenate(latents, axis=0)
            rope_ref[place, span, :] = jnp.concatenate(ropes, axis=0).astype(jnp.bfloat16)
    token = lax.broadcasted_iota(jnp.int32, (ARR * piece, heads), 0)
    position = token // piece * PAGE + share_index() * piece + lax.rem(token, piece)
    levels, shrinks, weights = [], [], []
    for load in query_loads:
        load.wait()
    for place in range(rows):
        query = query_refs[place]
        rope_query = jnp.concatenate([query[KVL:], query[KVL:]], axis=0)
        scores = jnp.dot(key_ref[place], query[:KVL], preferred_element_type=jnp.float32)
        scores += jnp.dot(rope_ref[place], rope_query, preferred_element_type=jnp.float32)
        scores = jnp.where(position < meta_ref[META_LEFT + place], SCORE_SCALE * scores, -jnp.inf)
        old_top, old_total = stat_ref[place : place + 1, :], stat_ref[MAXROWS + place : MAXROWS + place + 1, :]
        top = jnp.maximum(jnp.max(scores, axis=0, keepdims=True), old_top)
        shrink = jnp.exp(old_top - top)
        weight = jnp.exp(scores - top)
        total = jnp.sum(weight, axis=0, keepdims=True) + shrink * old_total
        inverse = 1.0 / total
        weights.append((weight * inverse).astype(jnp.bfloat16))
        shrinks.append(shrink * inverse)
        levels.append(top + jnp.log(total))
    columns = turned(stacked(shrinks))
    for load in loads[1:]:
        load.wait()
    even = lax.axis_index("core") == 0
    for place in range(rows):
        blend = blended(weights[place], key_ref[place])
        partial = (blend + columns[:, place : place + 1] * blend_refs[place]).astype(jnp.bfloat16)
        for chip in range(chips):
            block_even = partial[2 * chip * own : (2 * chip + 1) * own]
            block_odd = partial[(2 * chip + 1) * own : (2 * chip + 2) * own]
            block_mine = jnp.where(even, block_even, block_odd)
            block_other = jnp.where(even, block_odd, block_even)
            for chunk in range(KVL // 128):
                start = ((chip * (KVL // 128) + chunk) * rows + place) * own
                lanes = slice(chunk * 128, (chunk + 1) * 128)
                mine_ref[start : start + own, :] = block_mine[:, lanes]
                other_ref[start : start + own, :] = block_other[:, lanes]
    terms = coded(stacked(levels))
    stats = jnp.concatenate([terms[0][:rows], terms[1][:rows], terms[2][:rows], terms[0][rows:]], axis=0)
    stats = stats.astype(jnp.bfloat16)
    mine_ref[chips * (KVL // 128) * rows * own :, :] = stats
    other_ref[chips * (KVL // 128) * rows * own :, :] = stats


def merge_kernel(mine_ref, other_ref, handed_ref, send_ref, column_ref):
    chips = SHARES // 2
    rows, own = MAXROWS, (mine_ref.shape[0] - 16) // (chips * (KVL // 128) * MAXROWS)
    side = lax.axis_index("half")
    stat_base = chips * (KVL // 128) * rows * own
    level_a = decoded(mine_ref[stat_base:, :], rows)
    level_b = decoded(other_ref[stat_base:, :], rows)
    peak = jnp.maximum(level_a, level_b)
    weight_a, weight_b = jnp.exp(level_a - peak), jnp.exp(level_b - peak)
    total = weight_a + weight_b
    terms = coded(peak + jnp.log(total))
    inverse = 1.0 / total
    column_ref[...] = turned(jnp.concatenate([weight_a * inverse, weight_b * inverse], axis=0))
    core = lax.axis_index("core")
    stats = []
    for part in range(2):
        places = range(part * MOVES, (part + 1) * MOVES)
        kept = stacked([term[place : place + 1] for term in terms for place in places], 0, 16)
        stats.append((kept + handed_ref[...]).astype(jnp.bfloat16))
    for chip in range(chips):
        columns = column_ref[pl.ds(pl.multiple_of((2 * chip + core) * own, own), own), :]
        for part in range(2):
            target = jnp.where(side == part, PEERS.index(chips + chip), PEERS.index(chip))
            for move in range(MOVES):
                place = part * MOVES + move
                column_a = jnp.broadcast_to(columns[:, place : place + 1], (own, 128))
                column_b = jnp.broadcast_to(columns[:, rows + place : rows + place + 1], (own, 128))
                for chunk in range(KVL // 128):
                    start = ((chip * (KVL // 128) + chunk) * rows + place) * own
                    value = column_a * mine_ref[start : start + own, :].astype(jnp.float32)
                    value += column_b * other_ref[start : start + own, :].astype(jnp.float32)
                    to = (chunk * MOVES + move) * own
                    send_ref[target, to : to + own, :] = value.astype(jnp.bfloat16)
            send_ref[target, KVL // 128 * MOVES * own :, :] = stats[part]


def finish_kernel(received_ref, latent_ref, place_ref, out_ref, latent_out, column_ref):
    chips = SHARES // 2
    own = out_ref.shape[1]
    stat_base = KVL // 128 * MOVES * own
    side = lax.axis_index("half")
    sources, weights = [], []
    for part in range(2):
        sources.append(
            [jnp.where(side == part, PEERS.index(chips + chip), PEERS.index(chip)) for chip in range(chips)]
        )
        levels = [decoded(received_ref[source, stat_base:, :], MOVES) for source in sources[part]]
        peak = functools.reduce(jnp.maximum, levels)
        shares = [jnp.exp(level - peak) for level in levels]
        inverse = 1.0 / functools.reduce(lambda a, b: a + b, shares)
        weights.extend(share * inverse for share in shares)
    column_ref[...] = turned(jnp.concatenate(weights, axis=0))
    columns = column_ref[pl.ds(pl.multiple_of(share_index() * own, own), own), :]
    results = []
    for part in range(2):
        for move in range(MOVES):
            values = [0.0] * (KVL // 128)
            for chip in range(chips):
                lane = (part * chips + chip) * MOVES + move
                column = jnp.broadcast_to(columns[:, lane : lane + 1], (own, 128))
                for chunk in range(KVL // 128):
                    start = (chunk * MOVES + move) * own
                    block = received_ref[sources[part][chip], start : start + own, :].astype(jnp.float32)
                    values[chunk] = values[chunk] + column * block
            results.append(values)
    for row in range(MAXROWS):
        at = jnp.broadcast_to(place_ref[row : row + 1, :], (own, 128))
        for chunk in range(KVL // 128):
            value = results[MAXROWS - 1][chunk]
            for place in range(MAXROWS - 1):
                value = jnp.where(at == place, results[place][chunk], value)
            out_ref[row, :, chunk * 128 : (chunk + 1) * 128] = value.astype(jnp.bfloat16)
    taken = received_ref[sources[0][0], stat_base:, :].astype(jnp.float32)
    latent = latent_ref[...]
    rows, width = latent.shape
    at = jnp.concatenate([place_ref[:rows, :]] * LATENT_ROWS, axis=1)[:, :width]
    for move in range(MOVES):
        first = 3 * MOVES + move * LATENT_ROWS
        entry = jnp.concatenate([taken[first + chunk : first + chunk + 1] for chunk in range(LATENT_ROWS)], axis=1)
        latent = jnp.where(at == move, entry[:, :width], latent)
    latent_out[...] = latent.astype(jnp.bfloat16)


def shards(
    hidden,
    kva_weight,
    kv_gain,
    queries,
    latent_cache,
    outbox,
    out_dest,
    page_table,
    lengths,
    give_rows,
):
    group_count = lax.axis_size(DP)
    chip_count = lax.axis_size("x")
    row_count = hidden.shape[0]
    page_piece = latent_cache.shape[1]
    heads = queries.shape[1]
    own = heads // SHARES
    moves = give_rows.shape[0]
    query_t = jnp.swapaxes(queries, 1, 2)
    params = pltpu.CompilerParams(vmem_limit_bytes=VMEM_LIMIT)
    shape = jax.ShapeDtypeStruct
    in_hbm = functools.partial(pltpu.with_memory_space_constraint, memory_space=pltpu.HBM)

    outgoing = pl.pallas_call(
        pack_kernel,
        out_shape=shape((group_count, page_piece, CAP * (KVL + ROPE)), jnp.bfloat16),
        in_specs=[HBM(), HBM()],
        out_specs=ANY(),
        scratch_shapes=[
            pltpu.VMEM((outbox.shape[0] + 1,) + outbox.shape[1:], jnp.bfloat16),
            pltpu.VMEM((group_count, page_piece, CAP * (KVL + ROPE)), jnp.bfloat16),
            pltpu.SMEM(out_dest.shape, jnp.int32),
            pltpu.SMEM((group_count * CAP,), jnp.int32),
            pltpu.SemaphoreType.DMA((2,)),
            pltpu.SemaphoreType.DMA((4,)),
            pltpu.SemaphoreType.DMA,
        ],
        compiler_params=params,
        name="pack",
    )(in_hbm(out_dest), in_hbm(outbox))
    arrived = lax.all_to_all(outgoing, DP, split_axis=0, concat_axis=0, tiled=True, axis_index_groups=[ORDER])

    partial_raw = jnp.dot(hidden, kva_weight, preferred_element_type=jnp.float32)
    parts = lax.all_gather(partial_raw, TP)
    latent = lax.reduce_precision(normalize(jnp.sum(parts, axis=0), kv_gain), 8, 7)

    places = [0] * group_count
    for place, group in enumerate(ORDER):
        places[group] = place
    meta, stats, handed, place, *operands, blend = pl.pallas_call(
        resident_kernel,
        out_shape=(
            shape((128,), jnp.int32),
            shape((2 * MAXROWS, heads), jnp.float32),
            shape((16, 128), jnp.float32),
            shape((8, 128), jnp.int32),
        )
        + (shape(query_t.shape, jnp.bfloat16),)
        + (shape((row_count, heads, KVL), jnp.float32),),
        in_specs=[SMEM()] * 4 + [VMEM()] * 3,
        out_specs=(SMEM(),) + (VMEM(),) * 5,
        scratch_shapes=[pltpu.VMEM((row_count, RESMAX * page_piece + 16, latent_cache.shape[2]), jnp.bfloat16)],
        compiler_params=params,
        name="resident",
    )(give_rows, page_table, lengths, jnp.array(places, jnp.int32), latent_cache, query_t, latent)

    part_shape = shape((chip_count * (KVL // 128) * row_count * own + 16, 128), jnp.bfloat16)
    mine, other = pl.pallas_call(
        arrived_kernel,
        out_shape=(part_shape, part_shape),
        in_specs=[VMEM()] + [HBM()] * 2 + [VMEM()] * 2,
        out_specs=(VMEM(), VMEM()),
        scratch_shapes=[
            pltpu.VMEM((row_count, ARR * page_piece, KVL), jnp.bfloat16),
            pltpu.VMEM((row_count, ARR * page_piece, 128), jnp.bfloat16),
            pltpu.VMEM((row_count, heads, KVL), jnp.float32),
            pltpu.VMEM(query_t.shape, jnp.bfloat16),
            pltpu.SMEM((128,), jnp.int32),
            pltpu.SemaphoreType.DMA((2 * row_count + 1,)),
        ],
        compiler_params=params,
        name="arrived",
    )(meta, in_hbm(blend), in_hbm(operands[0]), arrived, stats)
    other = lax.ppermute(other, "core", [(0, 1), (1, 0)])
    outbound = pl.pallas_call(
        merge_kernel,
        out_shape=shape((2 * chip_count, KVL // 128 * moves * own + 16, 128), jnp.bfloat16),
        in_specs=[VMEM()] * 3,
        out_specs=VMEM(),
        scratch_shapes=[pltpu.VMEM((heads, 128), jnp.float32)],
        compiler_params=params,
        name="merge",
    )(mine, other, handed)
    received = lax.all_to_all(
        outbound, ("half", "x"), split_axis=0, concat_axis=0, tiled=True, axis_index_groups=[PEERS]
    )
    return pl.pallas_call(
        finish_kernel,
        out_shape=(
            shape((row_count, own, KVL), jnp.bfloat16),
            shape(latent.shape, jnp.bfloat16),
        ),
        in_specs=[VMEM()] * 3,
        out_specs=(VMEM(), VMEM()),
        scratch_shapes=[pltpu.VMEM((heads, 128), jnp.float32)],
        compiler_params=params,
        name="finish",
    )(received, latent, place)


def solution(mesh):
    groups, shares = mesh.devices.shape
    split = Mesh(mesh.devices.reshape(2, groups // 2, shares // 2, 2), DP + TP)
    placed = (
        P(DP, TP),
        P(TP, None),
        P(),
        P(DP, None, None),
        P(DP, TP, None),
        P(DP, TP, None),
        P(DP),
        P(DP, None),
        P(DP),
        P(DP),
    )
    return jax.shard_map(
        shards,
        mesh=split,
        in_specs=placed,
        out_specs=(P(DP, TP, None), P(DP, None)),
        check_vma=False,
    )
```
